256 devices in a mesh: leaf: 32 (over x, y, core), sep: 8 (over z).
Axes of the slice: x: 4, y: 4, z: 8, core: 2. Of those that a mesh axis runs over, the one named last changes fastest.
Arguments:
- leaf_rhs: bfloat16 [64, 32, 8, 256], P(None, 'leaf', 'sep'), may hold values from -6 to 6
- leaf_inv: bfloat16 [32, 8, 256, 256], P('leaf', 'sep'), as said below
- leaf_coupling: bfloat16 [32, 8, 256, 16128], P('leaf', 'sep')
- block_mask: int32 [32, 8, 126], P('leaf', 'sep'), may hold values 0 or 1
- leaf_rows: int32 [32, 8], P('leaf', 'sep'), may hold values from 1 to 256, 1280 in all within a row
- sep_rhs: bfloat16 [64, 32, 8, 192], P(None, 'leaf', 'sep'), may hold values from -6 to 6
- dinv_rows: float32 [32, 8, 32, 16128], P('leaf', 'sep'), as said below
- sep_coupling: float32 [32, 8, 32, 15872], P('leaf', 'sep')
Outputs:
- leaf_solution: bfloat16 [64, 32, 8, 256], P(None, 'leaf', 'sep')
- sep_solution: float32 [64, 32, 8, 192], P(None, 'leaf', 'sep')
The draws below stay inside these ranges and needn't reach their ends.
Inputs may be any that keep to these rules, and one draw needn't show every extreme that they name: leaf_inv[l, s, k, j] is 0 for k > j, and its diagonal lies in 0.6 to 1.6. dinv_rows holds rows of lower triangular matrices: entry (g, g') of a separator's block is 0 for g' > g, and its diagonal lies in 0.7 to 1.5.
All inputs are finite; a program needn't handle non-finite values. No bound on the sum of `block_mask` or of `leaf_rows` on one device may be relied on, other than what follows from the above.
Results may differ from the reference program's by a relative error of at most 0.0017.
Values sent between devices are 32-bit elements; how exact they have to be, the bound alone decides.
A program may use at most 64 MiB of HBM per device.

```python
import math
import jax
import jax.numpy as jnp
import numpy as np
from jax import lax

NRHS = 64
LR = 256
SR = 32
BLK = 128
LEVELS = 6
SUMS = 16128
PARCOLS = 15872
NBLK = 126
N_LEAF = 32
N_SEP = 8


def column_power(columns, base_rows):
    quotient = columns // base_rows + 1
    powers = jnp.ones_like(quotient)
    for step_idx in range(1, LEVELS):
        powers = jnp.where(quotient >= 2 ** step_idx, 2 ** step_idx, powers)
    return powers


def rough_values(key, full_shape, spread):
    return jax.random.normal(key, full_shape, jnp.float32) * spread


def draw_leaf_inv(key, part):
    key = jax.random.fold_in(key, 1)
    full_shape = (N_LEAF, N_SEP, LR, LR)
    values = rough_values(key, full_shape, 0.6 / math.sqrt(LR))
    diagonal = jax.random.uniform(jax.random.fold_in(key, 7), full_shape, jnp.float32, 0.6, 1.6)
    row_index = lax.broadcasted_iota(jnp.int32, full_shape, 2)
    col_index = lax.broadcasted_iota(jnp.int32, full_shape, 3)
    result = jnp.where(row_index < col_index, values, jnp.where(row_index == col_index, diagonal, 0.0))
    return result.astype(jnp.bfloat16)


def draw_leaf_coupling(key, part):
    key = jax.random.fold_in(key, 2)
    full_shape = (N_LEAF, N_SEP, LR, SUMS)
    col_index = lax.broadcasted_iota(jnp.int32, full_shape, 3)
    powers = column_power(col_index, SR * N_SEP)
    scales = 1.2 / jnp.sqrt((LR * N_SEP * powers).astype(jnp.float32))
    values = rough_values(key, full_shape, 1.0) * scales
    return values.astype(jnp.bfloat16)


def draw_dinv_rows(key, part):
    key = jax.random.fold_in(key, 3)
    full_shape = (N_LEAF, N_SEP, SR, SUMS)
    col_index = lax.broadcasted_iota(jnp.int32, full_shape, 3)
    leaf_index = lax.broadcasted_iota(jnp.int32, full_shape, 0)
    sep_index = lax.broadcasted_iota(jnp.int32, full_shape, 1)
    row_index = lax.broadcasted_iota(jnp.int32, full_shape, 2)
    powers = column_power(col_index, SR * N_SEP)
    local_col = col_index - SR * N_SEP * (powers - 1)
    global_row = (leaf_index % powers * N_SEP + sep_index) * SR + row_index
    scales = 0.7 / jnp.sqrt((SR * N_SEP * powers).astype(jnp.float32))
    values = rough_values(key, full_shape, 1.0) * scales
    diagonal = jax.random.uniform(jax.random.fold_in(key, 9), full_shape, jnp.float32, 0.7, 1.5)
    return jnp.where(local_col < global_row, values, jnp.where(local_col == global_row, diagonal, 0.0))


def draw_sep_coupling(key, part):
    key = jax.random.fold_in(key, 4)
    full_shape = (N_LEAF, N_SEP, SR, PARCOLS)
    col_index = lax.broadcasted_iota(jnp.int32, full_shape, 3)
    powers = column_power(col_index + SR * N_SEP, SR * N_SEP)
    scales = 0.8 / jnp.sqrt((SR * N_SEP * powers // 2).astype(jnp.float32))
    return rough_values(key, full_shape, 1.0) * scales


def with_ends(values, stream_key, least, largest):
    place = [jax.random.randint(jax.random.fold_in(stream_key, axis), (), 0, length) for axis, length in enumerate(values.shape)]
    longest = values.shape.index(max(values.shape))
    next_to = place[:longest] + [(place[longest] + 1) % values.shape[longest]] + place[longest + 1:]
    return values.at[tuple(place)].set(least).at[tuple(next_to)].set(largest)


def steps_of(rng, dims, shards, smallest, largest):
    level, own = 1.0, jax.random.fold_in(rng, 6)
    for position, parts in shards:
        draws = jnp.exp(jax.random.uniform(jax.random.fold_in(own, position), (parts,), jnp.float32, smallest / len(shards), largest / len(shards)))
        level = level * jnp.repeat(draws, dims[position] // parts).reshape([-1 if axis == position else 1 for axis in range(len(dims))])
    return level


def profile(number_of, total, reach, lean):
    weights = [(1 << 20) // math.isqrt(rank ** lean) + 1 for rank in range(2, number_of + 1)]
    surplus, given = total - reach - (number_of - 1), [1] * (number_of - 1)
    while surplus > 0:
        candidates = [i for i in range(number_of - 1) if given[i] < reach]
        whole, remaining = sum([weights[i] for i in candidates]), surplus
        for i in candidates:
            extra = min(reach - given[i], max(1, remaining * weights[i] // whole), surplus)
            given[i] = given[i] + extra
            surplus = surplus - extra
    return np.array([reach] + given)


def ragged(key, amount, total, reach, slope):
    if amount == 2:
        one = jax.random.randint(key, (), max(1, total - reach), min(reach, total - 1) + 1)
        return jnp.stack([one, total - one])
    tallies = jnp.asarray(profile(amount, total, reach, slope), jnp.int32)
    pairs = (amount - 1) // 2
    source_of, sink = tallies[1:1 + 2 * pairs:2], tallies[2:2 + 2 * pairs:2]
    room = jnp.minimum(source_of - 1, reach - sink)
    shifted = jax.random.randint(jax.random.fold_in(key, 1), (pairs,), 0, 1 << 20) % (room + 1)
    tallies = tallies.at[1:1 + 2 * pairs:2].set(source_of - shifted).at[2:2 + 2 * pairs:2].set(sink + shifted)
    return tallies[jax.random.permutation(jax.random.fold_in(key, 2), amount)]


def scatter_about(own_key, dims, scale, bound, cuts=(), held_as=jnp.bfloat16):
    loudness = steps_of(own_key, dims, cuts, -0.22, 0.18) if cuts else 1.0
    entries = jax.random.normal(own_key, dims, jnp.float32) * scale * loudness
    return jnp.minimum(jnp.maximum(entries, -bound), bound).astype(held_as)


def setup_inputs(seed: int = 0) -> dict:
    key_of = jax.random.split(jax.random.key(seed), 9)
    return {
        "leaf_rhs": scatter_about(key_of[0], (NRHS, N_LEAF, N_SEP, LR), 1.0, 6.0, ((1, 32), (2, 8))),
        "leaf_inv": draw_leaf_inv(jax.random.fold_in(key_of[8], 71), 0),
        "leaf_coupling": draw_leaf_coupling(jax.random.fold_in(key_of[8], 71), 0),
        "block_mask": with_ends((jax.random.randint(key_of[3], (N_LEAF, N_SEP, NBLK), 0, 2) < 1).astype(jnp.int32), jax.random.fold_in(key_of[3], 1), 0, 1),
        "leaf_rows": jax.vmap(lambda own: ragged(own, N_SEP, N_SEP * LR * 5 // 8, LR, 1))(jax.random.split(key_of[4], N_LEAF)).reshape((N_LEAF, N_SEP)).astype(jnp.int32),
        "sep_rhs": scatter_about(key_of[5], (NRHS, N_LEAF, N_SEP, LEVELS * SR), 1.0, 6.0, ((1, 32), (2, 8))),
        "dinv_rows": draw_dinv_rows(jax.random.fold_in(key_of[8], 71), 0),
        "sep_coupling": draw_sep_coupling(jax.random.fold_in(key_of[8], 71), 0),
    }


def reference(leaf_rhs, leaf_inv, leaf_coupling, block_mask, leaf_rows, sep_rhs, dinv_rows, sep_coupling):
    row_ids = jnp.arange(LR, dtype=jnp.int32)
    live_rows = row_ids[None, None, :] < leaf_rows[:, :, None]
    masked = jnp.where(live_rows[None], leaf_rhs, jnp.zeros_like(leaf_rhs))

    def leaf_solve(index):
        right_side = masked[:, index].astype(jnp.float32)
        inverse = leaf_inv[index].astype(jnp.float32)
        return jnp.einsum('rsk,skj->rsj', right_side, inverse)

    solved = lax.map(leaf_solve, jnp.arange(N_LEAF, dtype=jnp.int32))
    solved = jnp.moveaxis(solved, 0, 1)
    leaf_solution = jnp.where(live_rows[None], solved, jnp.zeros_like(solved)).astype(jnp.bfloat16)
    column_mask = jnp.repeat(block_mask, BLK, axis=2).astype(jnp.float32)
    base_rows = SR * N_SEP
    outputs = []
    carried = None
    for level_idx in range(LEVELS):
        members = 2 ** level_idx
        seg_width = base_rows * members
        offset = base_rows * (members - 1)

        def leaf_terms(index):
            values = leaf_solution[:, index].astype(jnp.float32)
            weights = lax.dynamic_slice_in_dim(leaf_coupling[index], offset, seg_width, 2).astype(jnp.float32)
            masks = lax.dynamic_slice_in_dim(column_mask[index], offset, seg_width, 1)
            products = jnp.einsum('rsk,skj->srj', values, weights)
            return products * masks[:, None, :]

        terms = lax.map(leaf_terms, jnp.arange(N_LEAF, dtype=jnp.int32))
        grouped = terms.reshape(N_LEAF // members, members, N_SEP, NRHS, seg_width).sum(axis=(1, 2))
        pieces = sep_rhs[:, :, :, level_idx * SR:(level_idx + 1) * SR].astype(jnp.float32)
        pieces = pieces.reshape(NRHS, N_LEAF // members, seg_width)
        residual = jnp.moveaxis(pieces, 0, 1) - grouped
        if carried is not None:
            residual = residual - carried
        spread = jnp.repeat(residual, members, axis=0)
        inverse = dinv_rows[:, :, :, offset:offset + seg_width]
        solved_sep = jnp.einsum('lru,lsiu->lsri', spread, inverse, precision=lax.Precision.HIGHEST)
        outputs.append(solved_sep)
        if level_idx < LEVELS - 1:
            parent_start = base_rows * (2 * members - 2)
            couple = sep_coupling[:, :, :, parent_start:parent_start + 2 * seg_width]
            contrib = jnp.einsum('lsri,lsij->lsrj', solved_sep, couple, precision=lax.Precision.HIGHEST)
            carried = contrib.reshape(N_LEAF // (2 * members), 2 * members, N_SEP, NRHS, 2 * seg_width).sum(axis=(1, 2))
    stacked = jnp.stack(outputs, axis=0)
    stacked = jnp.transpose(stacked, (3, 1, 2, 0, 4))
    sep_solution = stacked.reshape(NRHS, N_LEAF, N_SEP, LEVELS * SR)
    return leaf_solution, sep_solution
```

```python
import functools

import jax
import jax.numpy as jnp
from jax import lax
from jax.experimental import pallas as pl
from jax.experimental.pallas import tpu as pltpu
from jax.sharding import PartitionSpec as P

MESH = pl.DeviceIdType.MESH
LEVELS = 6
SEPS = 8
RHS = 64
CH = 256
F32 = jnp.float32
BF16 = jnp.bfloat16


def first_chunk(v):
    return 2**v - 1


def xy_slot(v):
    return sum(2 ** (u - 1) - 1 for u in range(2, v))


def core_slot(v):
    return 2 ** (v - 1) - 1


def split(x):
    hi = x.astype(BF16)
    lo = (x - hi.astype(F32)).astype(BF16)
    return hi, lo


def kernel(
    mask_ref, rows_ref, rhs_ref, inv_ref, srhs_ref, coup_hbm, dinv_hbm, scoup_hbm,
    leaf_out, sep_out,
    weights, dfull, cfull, dstack, cstack, part, core_in, xy_in, z_out, z_in, resid, sol_ref,
    sem_w, sem_d, sem_c,
    zr_s, zr_r, zg_s, zg_r, xr_s, xr_r, xg_s, xg_r, cr_s, cr_r, cg_s, cg_r,
):
    leaf = lax.axis_index("leaf")
    sep = lax.axis_index("sep")
    core = lax.rem(leaf, 2)
    other = 1 - core
    bits = [lax.rem(leaf // 2 ** (k + 1), 2) for k in range(4)]
    partner = leaf + 1 - 2 * core

    def xy_of(v):
        return lax.rem(leaf // 2, 2 ** (v - 1))

    def flip(d):
        return sum(2**k * (1 - 2 * bits[k]) for k in range(4) if d >> k & 1)

    def place(v, which_core, xy):
        if v == 0:
            return 0
        return first_chunk(v) + which_core * 2 ** (v - 1) + xy

    def mine(v):
        return 0 if v == 0 else place(v, core, xy_of(v))

    def column(v, which_core, xy):
        if v == 0:
            return 0
        return pl.multiple_of((first_chunk(v) + 2 * xy + which_core) * CH, CH)

    def peers(v):
        return range(1, 2 ** (v - 1)) if v >= 2 else range(0)

    def level_cols(v):
        return pl.ds(first_chunk(v) * CH, 2**v * CH)

    def parent_cols(v):
        return pl.ds((first_chunk(v) - 1) * CH, 2**v * CH)

    def load_w(v):
        return pltpu.make_async_copy(
            coup_hbm.at[:, level_cols(v)], weights.at[:, level_cols(v)], sem_w.at[v])

    def load_d(v):
        return pltpu.make_async_copy(
            dinv_hbm.at[:, level_cols(v)], dfull.at[:, level_cols(v)], sem_d.at[v])

    def load_c(v):
        return pltpu.make_async_copy(
            scoup_hbm.at[:, parent_cols(v)], cfull.at[:, parent_cols(v)], sem_c.at[v])

    def remote(src, dst, send, recv, to):
        return pltpu.make_async_remote_copy(
            src_ref=src, dst_ref=dst, send_sem=send, recv_sem=recv,
            device_id=to, device_id_type=MESH)

    def z_peer(d):
        return lax.rem(sep + d, SEPS)

    def zr(v, d):
        return remote(z_out.at[v, z_peer(d)], z_in.at[v, d - 1],
                      zr_s.at[v, d - 1], zr_r.at[v, d - 1], (leaf, z_peer(d)))

    def zg(v, d):
        return remote(resid.at[mine(v), sep], resid.at[mine(v), sep],
                      zg_s.at[v, d - 1], zg_r.at[v, d - 1], (leaf, z_peer(d)))

    def zg_in(v, d):
        src = z_peer(SEPS - d)
        return remote(resid.at[mine(v), src], resid.at[mine(v), src],
                      zg_s.at[v, d - 1], zg_r.at[v, d - 1], (leaf, z_peer(d)))

    def xr(v, d):
        k = xy_slot(v) + d - 1
        return remote(part.at[place(v, core, xy_of(v) + flip(d))], xy_in.at[k],
                      xr_s.at[k], xr_r.at[k], (leaf + 2 * flip(d), sep))

    def xg(v, d, incoming=False):
        k = xy_slot(v) + d - 1
        at = place(v, core, xy_of(v) + (flip(d) if incoming else 0))
        return remote(resid.at[at], resid.at[at],
                      xg_s.at[k], xg_r.at[k], (leaf + 2 * flip(d), sep))

    def cr(v, i):
        k = core_slot(v) + i
        return remote(part.at[place(v, other, i)], core_in.at[k],
                      cr_s.at[k], cr_r.at[k], (partner, sep))

    def cg(v, d, incoming=False):
        k = core_slot(v) + d
        at = place(v, other if incoming else core, xy_of(v) + flip(d))
        return remote(resid.at[at], resid.at[at],
                      cg_s.at[k], cg_r.at[k], (partner, sep))

    for v in range(LEVELS):
        load_w(v).start()
        load_d(v).start()
        if v:
            load_c(v).start()

    barrier = pltpu.get_barrier_semaphore()
    pl.semaphore_signal(barrier, inc=1, device_id=(partner, sep), device_id_type=MESH)
    for d in range(1, 16):
        pl.semaphore_signal(
            barrier, inc=1, device_id=(leaf + 2 * flip(d), sep), device_id_type=MESH)
    for d in range(1, SEPS):
        pl.semaphore_signal(
            barrier, inc=1, device_id=(leaf, z_peer(d)), device_id_type=MESH)

    live = lax.broadcasted_iota(jnp.int32, (RHS, CH), 1) < rows_ref[0, 0]
    right = jnp.where(live, rhs_ref[...].astype(F32), 0.0).astype(BF16)
    solved = jnp.dot(right, inv_ref[...], preferred_element_type=F32)
    solved = jnp.where(live, solved, 0.0).astype(BF16)
    sol_ref[...] = solved
    leaf_out[...] = solved

    def terms_chunk(v, which_core, xy):
        m = 0 if v == 0 else 2 * xy + which_core
        block = 2 * (first_chunk(v) + m)
        col = column(v, which_core, xy)
        t = jnp.dot(sol_ref[...], weights[:, pl.ds(col, CH)], preferred_element_type=F32)
        left = t[:, :128] * (-mask_ref[block].astype(F32))
        rest = t[:, 128:] * (-mask_ref[block + 1].astype(F32))
        t = jnp.concatenate([left, rest], axis=1)
        part[place(v, which_core, xy)] = t.reshape(SEPS, 8, CH)

    def terms(v):
        load_w(v).wait()
        if v == 0:
            terms_chunk(0, 0, 0)
        else:
            n = 2 ** (v - 1)
            step = min(n, 2)

            def some(i, carry):
                for j in range(step):
                    for c in range(2):
                        terms_chunk(v, c, i * step + j)
                return carry

            if n == step:
                some(0, 0)
            else:
                lax.fori_loop(0, n // step, some, 0)
        r = lax.broadcasted_iota(jnp.int32, (LEVELS * 32, CH), 0)
        c = lax.broadcasted_iota(jnp.int32, (LEVELS * 32, CH), 1)
        pick = jnp.where((r - 32 * v == c - 32 * sep) & (r >= 32 * v) & (r < 32 * v + 32), 1.0, 0.0)
        own = jnp.dot(srhs_ref[...], pick.astype(BF16), preferred_element_type=F32)
        at = mine(v)
        part[at] = part[at] + own.reshape(SEPS, 8, CH)

    def stack(src, dst, start, size):
        cols = pl.ds(pl.multiple_of(start, CH), size)
        hi, lo = split(src[:, cols])
        dst[0:32, cols] = hi
        dst[32:64, cols] = lo
        dst[64:96, cols] = hi
        dst[96:128, cols] = lo

    def stack_all(src, dst, start, size):
        width = min(size, 512)
        if size == width:
            stack(src, dst, start, size)
        else:
            def some(i, carry):
                stack(src, dst, start + i * width, width)
                return carry
            lax.fori_loop(0, size // width, some, 0)

    def prep(v):
        load_d(v).wait()
        stack_all(dfull, dstack, first_chunk(v) * CH, 2**v * CH)
        if v:
            load_c(v).wait()
            stack_all(cfull, cstack, (first_chunk(v) - 1) * CH, 2**v * CH)

    lanes = lax.broadcasted_iota(jnp.int32, (RHS, 128), 1)

    def product(v, which_core, xy, at, acc):
        hi, lo = split(resid[at].reshape(RHS, CH))
        rows = jnp.concatenate([hi, lo], axis=0)
        col = column(v, which_core, xy)
        return acc + lax.dot_general(
            rows, dstack[:, pl.ds(col, CH)], (((1,), (1,)), ((), ())),
            preferred_element_type=F32)

    def couple_chunk(v, xs, which_core, xy):
        at = place(v, which_core, xy)
        col = (first_chunk(v) - 1 + 2 * xy + which_core) * CH
        t = jnp.dot(xs, cstack[:, pl.ds(pl.multiple_of(col, CH), CH)], preferred_element_type=F32)
        part[at] = part[at] - t.reshape(SEPS, 8, CH)

    terms(0)
    z_out[0] = part[0]
    pl.semaphore_wait(barrier, 1 + 15 + 7)

    for v in range(LEVELS):
        if v >= 1:
            n = 2 ** (v - 1)
            step = min(n, 4)

            def theirs(i, carry):
                for j in range(step):
                    couple_chunk(v, xs, other, i * step + j)
                    cr(v, i * step + j).start()
                return carry

            def ours(i, carry):
                for j in range(step):
                    couple_chunk(v, xs, core, i * step + j)
                return carry

            if n == step:
                theirs(0, 0)
                ours(0, 0)
            else:
                lax.fori_loop(0, n // step, theirs, 0)
                lax.fori_loop(0, n // step, ours, 0)
            for d in peers(v):
                i = xy_of(v) + flip(d)
                cr(v, i).wait_recv()
                at = place(v, core, i)
                part[at] = part[at] + core_in[core_slot(v) + i]
                xr(v, d).start()
            i = xy_of(v)
            cr(v, i).wait_recv()
            total = part[mine(v)] + core_in[core_slot(v) + i]
            for d in peers(v):
                xr(v, d).wait_recv()
                total = total + xy_in[xy_slot(v) + d - 1]
            z_out[v] = total
        for d in range(1, SEPS):
            zr(v, d).start()
        if v == 0:
            prep(0)
            terms(1)
            prep(1)
            terms(2)
        elif v < LEVELS - 1:
            prep(v + 1)
        if v >= 1:
            for i in range(2 ** (v - 1)):
                cr(v, i).wait_send()
            for d in peers(v):
                xr(v, d).wait_send()
        total = z_out[v, sep]
        for d in range(1, SEPS):
            zr(v, d).wait_recv()
            total = total + z_in[v, d - 1]
        resid[mine(v), sep] = total
        for d in range(1, SEPS):
            zg(v, d).start()
        if v + 3 < LEVELS:
            terms(v + 3)
        for d in range(1, SEPS):
            zr(v, d).wait_send()
        for d in range(1, SEPS):
            zg_in(v, d).wait_recv()
        if v >= 1:
            cg(v, 0).start()
            for d in peers(v):
                xg(v, d).start()
        acc = jnp.zeros((2 * RHS, 128), F32)
        if v == 0:
            acc = product(0, 0, 0, 0, acc)
        else:
            acc = product(v, core, xy_of(v), mine(v), acc)
            for d in peers(v):
                xg(v, d, True).wait_recv()
                cg(v, d).start()
                i = xy_of(v) + flip(d)
                acc = product(v, core, i, place(v, core, i), acc)
            for d in range(2 ** (v - 1)):
                cg(v, d, True).wait_recv()
                i = xy_of(v) + flip(d)
                acc = product(v, other, i, place(v, other, i), acc)
        t = acc[:RHS] + acc[RHS:]
        x = t + pltpu.roll(t, 32, 1)
        if v < 4:
            old = jnp.zeros_like(x) if v == 0 else sep_out[:, :128]
            sep_out[:, :128] = jnp.where(lanes // 32 == v, x, old)
        else:
            sep_out[:, 32 * v : 32 * v + 32] = x[:, 32 * (v - 4) : 32 * (v - 3)]
        hi, lo = split(x)
        xs = jnp.where(lanes < 64, hi.astype(F32), lo.astype(F32)).astype(BF16)
        for d in range(1, SEPS):
            zg(v, d).wait_send()
        if v >= 1:
            for d in range(2 ** (v - 1)):
                cg(v, d).wait_send()
            for d in peers(v):
                xg(v, d).wait_send()


def body(
    leaf_rhs, leaf_inv, leaf_coupling, block_mask, leaf_rows, sep_rhs, dinv_rows, sep_coupling
):
    sums = leaf_coupling.shape[3]
    parents = sep_coupling.shape[3]
    dma = pltpu.SemaphoreType.DMA
    vmem = pl.BlockSpec(memory_space=pltpu.VMEM)
    smem = pl.BlockSpec(memory_space=pltpu.SMEM)
    hbm = pl.BlockSpec(memory_space=pl.ANY)
    leaf_solution, sep_solution = pl.pallas_call(
        kernel,
        out_shape=(
            jax.ShapeDtypeStruct((RHS, CH), BF16),
            jax.ShapeDtypeStruct((RHS, LEVELS * 32), F32),
        ),
        in_specs=[smem, smem, vmem, vmem, vmem, hbm, hbm, hbm],
        out_specs=(vmem, vmem),
        scratch_shapes=[
            pltpu.VMEM((CH, sums), BF16),
            pltpu.VMEM((32, sums), F32),
            pltpu.VMEM((32, parents), F32),
            pltpu.VMEM((128, sums), BF16),
            pltpu.VMEM((128, parents), BF16),
            pltpu.VMEM((63, SEPS, 8, CH), F32),
            pltpu.VMEM((31, SEPS, 8, CH), F32),
            pltpu.VMEM((26, SEPS, 8, CH), F32),
            pltpu.VMEM((LEVELS, SEPS, 8, CH), F32),
            pltpu.VMEM((LEVELS, SEPS - 1, 8, CH), F32),
            pltpu.VMEM((63, SEPS, 8, CH), F32),
            pltpu.VMEM((RHS, CH), BF16),
            dma((LEVELS,)), dma((LEVELS,)), dma((LEVELS,)),
            dma((LEVELS, 7)), dma((LEVELS, 7)), dma((LEVELS, 7)), dma((LEVELS, 7)),
            dma((26,)), dma((26,)), dma((26,)), dma((26,)),
            dma((31,)), dma((31,)), dma((31,)), dma((31,)),
        ],
        compiler_params=pltpu.CompilerParams(
            collective_id=0, has_side_effects=True, vmem_limit_bytes=60 * 2**20),
        name="forward_substitution",
    )(
        block_mask[0, 0], leaf_rows, leaf_rhs[:, 0, 0, :], leaf_inv[0, 0], sep_rhs[:, 0, 0, :],
        leaf_coupling[0, 0], dinv_rows[0, 0], sep_coupling[0, 0],
    )
    return (leaf_solution[:, None, None, :], sep_solution[:, None, None, :])


def solution(mesh):
    return jax.shard_map(
        body,
        mesh=mesh,
        in_specs=(
            P(None, "leaf", "sep", None),
            P("leaf", "sep", None, None),
            P("leaf", "sep", None, None),
            P("leaf", "sep", None),
            P("leaf", "sep"),
            P(None, "leaf", "sep", None),
            P("leaf", "sep", None, None),
            P("leaf", "sep", None, None),
        ),
        out_specs=(P(None, "leaf", "sep", None), P(None, "leaf", "sep", None)),
        check_vma=False,
    )
```

```python
import functools

import jax
import jax.numpy as jnp
from jax import lax
from jax.experimental import pallas as pl
from jax.experimental.pallas import tpu as pltpu
from jax.sharding import PartitionSpec as P

MESH = pl.DeviceIdType.MESH
LEVELS = 6
TOP = LEVELS - 1
TOP_CHUNKS = 4
SEPS = 8
RHS = 64
CH = 256
F32 = jnp.float32
BF16 = jnp.bfloat16


def first_chunk(v):
    return 2**v - 1


def xy_slot(v):
    return sum(2 ** (u - 1) - 1 for u in range(2, v))


def core_slot(v):
    return 2 ** (v - 1) - 1


def split(x):
    hi = x.astype(BF16)
    lo = (x - hi.astype(F32)).astype(BF16)
    return hi, lo


def kernel(
    mask_ref, rows_ref, rhs_ref, inv_ref, srhs_ref, coup_hbm, dinv_hbm, scoup_hbm,
    leaf_out, sep_out,
    weights, dfull, cfull, dstack, cstack, part, core_in, xy_in, z_out, z_in, resid, sol_ref,
    wide_in, wide_hi, wide_lo, x_all, tiles, tiles_core, tiles_xy, tiles_res, x_out, x_in,
    sem_w, sem_d, sem_c,
    zr_s, zr_r, zg_s, zg_r, xr_s, xr_r, xg_s, xg_r, cr_s, cr_r, cg_s, cg_r,
    wz_s, wz_r, xa_s, xa_r, uc_s, uc_r, ux_s, ux_r, tg_s, tg_r, tc_s, tc_r, xo_s, xo_r,
):
    leaf = lax.axis_index("leaf")
    sep = lax.axis_index("sep")
    core = lax.rem(leaf, 2)
    other = 1 - core
    bits = [lax.rem(leaf // 2 ** (k + 1), 2) for k in range(4)]
    partner = leaf + 1 - 2 * core

    def xy_of(v):
        return lax.rem(leaf // 2, 2 ** (v - 1))

    def flip(d):
        return sum(2**k * (1 - 2 * bits[k]) for k in range(4) if d >> k & 1)

    def place(v, which_core, xy):
        if v == 0:
            return 0
        return first_chunk(v) + which_core * 2 ** (v - 1) + xy

    def mine(v):
        return 0 if v == 0 else place(v, core, xy_of(v))

    def column(v, which_core, xy):
        if v == 0:
            return 0
        return pl.multiple_of((first_chunk(v) + 2 * xy + which_core) * CH, CH)

    def peers(v):
        return range(1, 2 ** (v - 1)) if v >= 2 else range(0)

    def level_cols(v):
        return pl.ds(first_chunk(v) * CH, 2**v * CH)

    def parent_cols(v):
        return pl.ds((first_chunk(v) - 1) * CH, 2**v * CH)

    def load_w(v):
        return pltpu.make_async_copy(
            coup_hbm.at[:, level_cols(v)], weights.at[:, level_cols(v)], sem_w.at[v])

    def load_d(v):
        return pltpu.make_async_copy(
            dinv_hbm.at[:, level_cols(v)], dfull.at[:, level_cols(v)], sem_d.at[v])

    def load_c(v):
        return pltpu.make_async_copy(
            scoup_hbm.at[:, parent_cols(v)], cfull.at[:, parent_cols(v)], sem_c.at[v])

    def remote(src, dst, send, recv, to):
        return pltpu.make_async_remote_copy(
            src_ref=src, dst_ref=dst, send_sem=send, recv_sem=recv,
            device_id=to, device_id_type=MESH)

    def z_peer(d):
        return lax.rem(sep + d, SEPS)

    def zr(v, d):
        return remote(z_out.at[v, z_peer(d)], z_in.at[v, d - 1],
                      zr_s.at[v, d - 1], zr_r.at[v, d - 1], (leaf, z_peer(d)))

    def zg(v, d):
        return remote(resid.at[mine(v), sep], resid.at[mine(v), sep],
                      zg_s.at[v, d - 1], zg_r.at[v, d - 1], (leaf, z_peer(d)))

    def zg_in(v, d):
        src = z_peer(SEPS - d)
        return remote(resid.at[mine(v), src], resid.at[mine(v), src],
                      zg_s.at[v, d - 1], zg_r.at[v, d - 1], (leaf, z_peer(d)))

    def xr(v, d):
        k = xy_slot(v) + d - 1
        return remote(part.at[place(v, core, xy_of(v) + flip(d))], xy_in.at[k],
                      xr_s.at[k], xr_r.at[k], (leaf + 2 * flip(d), sep))

    def xg(v, d, incoming=False):
        k = xy_slot(v) + d - 1
        at = place(v, core, xy_of(v) + (flip(d) if incoming else 0))
        return remote(resid.at[at], resid.at[at],
                      xg_s.at[k], xg_r.at[k], (leaf + 2 * flip(d), sep))

    def cr(v, i):
        k = core_slot(v) + i
        return remote(part.at[place(v, other, i)], core_in.at[k],
                      cr_s.at[k], cr_r.at[k], (partner, sep))

    def cg(v, d, incoming=False):
        k = core_slot(v) + d
        at = place(v, other if incoming else core, xy_of(v) + flip(d))
        return remote(resid.at[at], resid.at[at],
                      cg_s.at[k], cg_r.at[k], (partner, sep))

    def wide(a, d, incoming=False):
        src, first = ((cfull, first_chunk(TOP) - 1), (dfull, first_chunk(TOP)))[a]
        to = z_peer(d)
        cols = pl.ds(pl.multiple_of((first + to * TOP_CHUNKS) * CH, CH), TOP_CHUNKS * CH)
        at = z_peer(SEPS - d) if incoming else sep
        return remote(src.at[:, cols], wide_in.at[a, at],
                      wz_s.at[a, d - 1], wz_r.at[a, d - 1], (leaf, to))

    def fire(pieces):
        for a, d in pieces:
            wide(a, d).start()

    def wide_stack(a, at, block):
        rows = pl.ds(pl.multiple_of(at * 32, 32), 32)
        hi, lo = split(block)
        wide_hi[a, rows, :] = hi
        wide_lo[a, rows, :] = lo

    def wide_prep(a):
        src, first = ((cfull, first_chunk(TOP) - 1), (dfull, first_chunk(TOP)))[a]
        cols = pl.ds(pl.multiple_of((first + sep * TOP_CHUNKS) * CH, CH), TOP_CHUNKS * CH)
        wide_stack(a, sep, src[:, cols])
        for d in range(1, SEPS):
            wide(a, d, True).wait_recv()
            at = z_peer(SEPS - d)
            wide_stack(a, at, wide_in[a, at])

    def xa(d, incoming=False):
        at = z_peer(SEPS - d) if incoming else sep
        return remote(x_all.at[at], x_all.at[at], xa_s.at[d - 1], xa_r.at[d - 1],
                      (leaf, z_peer(d)))

    def uc():
        return remote(tiles.at[other], tiles_core, uc_s.at[0], uc_r.at[0], (partner, sep))

    def ux(d):
        return remote(tiles.at[core, xy_of(TOP) + flip(d)], tiles_xy.at[d - 1],
                      ux_s.at[d - 1], ux_r.at[d - 1], (leaf + 2 * flip(d), sep))

    def tg(d, incoming=False):
        at = xy_of(TOP) + (flip(d) if incoming else 0)
        return remote(tiles_res.at[core, at], tiles_res.at[core, at],
                      tg_s.at[d - 1], tg_r.at[d - 1], (leaf + 2 * flip(d), sep))

    def tc(d, incoming=False):
        which = other if incoming else core
        at = xy_of(TOP) + flip(d)
        return remote(tiles_res.at[which, at], tiles_res.at[which, at],
                      tc_s.at[d], tc_r.at[d], (partner, sep))

    def xo(d):
        return remote(x_out.at[z_peer(d)], x_in.at[d - 1], xo_s.at[d - 1], xo_r.at[d - 1],
                      (leaf, z_peer(d)))

    for v in range(LEVELS):
        load_w(v).start()
        load_d(v).start()
        if v:
            load_c(v).start()

    barrier = pltpu.get_barrier_semaphore()
    pl.semaphore_signal(barrier, inc=1, device_id=(partner, sep), device_id_type=MESH)
    for d in range(1, 16):
        pl.semaphore_signal(
            barrier, inc=1, device_id=(leaf + 2 * flip(d), sep), device_id_type=MESH)
    for d in range(1, SEPS):
        pl.semaphore_signal(
            barrier, inc=1, device_id=(leaf, z_peer(d)), device_id_type=MESH)

    live = lax.broadcasted_iota(jnp.int32, (RHS, CH), 1) < rows_ref[0, 0]
    right = jnp.where(live, rhs_ref[...].astype(F32), 0.0).astype(BF16)
    solved = jnp.dot(right, inv_ref[...], preferred_element_type=F32)
    solved = jnp.where(live, solved, 0.0).astype(BF16)
    sol_ref[...] = solved
    leaf_out[...] = solved

    def terms_chunk(v, which_core, xy):
        m = 0 if v == 0 else 2 * xy + which_core
        block = 2 * (first_chunk(v) + m)
        col = column(v, which_core, xy)
        t = jnp.dot(sol_ref[...], weights[:, pl.ds(col, CH)], preferred_element_type=F32)
        left = t[:, :128] * (-mask_ref[block].astype(F32))
        rest = t[:, 128:] * (-mask_ref[block + 1].astype(F32))
        t = jnp.concatenate([left, rest], axis=1)
        part[place(v, which_core, xy)] = t.reshape(SEPS, 8, CH)

    def own_rows(v):
        r = lax.broadcasted_iota(jnp.int32, (LEVELS * 32, CH), 0)
        c = lax.broadcasted_iota(jnp.int32, (LEVELS * 32, CH), 1)
        pick = jnp.where((r - 32 * v == c - 32 * sep) & (r >= 32 * v) & (r < 32 * v + 32), 1.0, 0.0)
        own = jnp.dot(srhs_ref[...], pick.astype(BF16), preferred_element_type=F32)
        return own.reshape(SEPS, 8, CH)

    def tile_place(j, g):
        return first_chunk(TOP) + (g % 2) * 2 ** (TOP - 1) + j * 4 + g // 2

    def top_terms():
        load_w(TOP).wait()

        def some(at, carry):
            for j in range(TOP_CHUNKS):
                m = at * TOP_CHUNKS + j
                block = 2 * (first_chunk(TOP) + m)
                col = pl.multiple_of((first_chunk(TOP) + m) * CH, CH)
                t = jnp.dot(sol_ref[...], weights[:, pl.ds(col, CH)], preferred_element_type=F32)
                left = t[:, :128] * (-mask_ref[block].astype(F32))
                rest = t[:, 128:] * (-mask_ref[block + 1].astype(F32))
                t = jnp.concatenate([left, rest], axis=1)
                for g in range(8):
                    part[tile_place(j, g), at] = t[8 * g : 8 * g + 8]
            return carry

        lax.fori_loop(0, SEPS, some, 0)
        own = own_rows(TOP)
        at = leaf // TOP_CHUNKS
        j = lax.rem(leaf, TOP_CHUNKS)
        for g in range(8):
            k = tile_place(j, g)
            part[k, at] = part[k, at] + own[g]

    def terms(v):
        load_w(v).wait()
        if v == 0:
            terms_chunk(0, 0, 0)
        else:
            n = 2 ** (v - 1)
            step = min(n, 2)

            def some(i, carry):
                for j in range(step):
                    for c in range(2):
                        terms_chunk(v, c, i * step + j)
                return carry

            if n == step:
                some(0, 0)
            else:
                lax.fori_loop(0, n // step, some, 0)
        at = mine(v)
        part[at] = part[at] + own_rows(v)

    def stack(src, dst, start, size):
        cols = pl.ds(pl.multiple_of(start, CH), size)
        hi, lo = split(src[:, cols])
        dst[0:32, cols] = hi
        dst[32:64, cols] = lo
        dst[64:96, cols] = hi
        dst[96:128, cols] = lo

    def stack_all(src, dst, start, size):
        width = min(size, 512)
        if size == width:
            stack(src, dst, start, size)
        else:
            def some(i, carry):
                stack(src, dst, start + i * width, width)
                return carry
            lax.fori_loop(0, size // width, some, 0)

    def prep(v):
        load_d(v).wait()
        stack_all(dfull, dstack, first_chunk(v) * CH, 2**v * CH)
        if v:
            load_c(v).wait()
            stack_all(cfull, cstack, (first_chunk(v) - 1) * CH, 2**v * CH)

    lanes = lax.broadcasted_iota(jnp.int32, (RHS, 128), 1)

    def product(v, which_core, xy, at, acc):
        hi, lo = split(resid[at].reshape(RHS, CH))
        rows = jnp.concatenate([hi, lo], axis=0)
        col = column(v, which_core, xy)
        return acc + lax.dot_general(
            rows, dstack[:, pl.ds(col, CH)], (((1,), (1,)), ((), ())),
            preferred_element_type=F32)

    def couple_chunk(v, xs, which_core, xy):
        at = place(v, which_core, xy)
        col = (first_chunk(v) - 1 + 2 * xy + which_core) * CH
        t = jnp.dot(xs, cstack[:, pl.ds(pl.multiple_of(col, CH), CH)], preferred_element_type=F32)
        part[at] = part[at] - t.reshape(SEPS, 8, CH)

    terms(0)
    z_out[0] = part[0]
    pl.semaphore_wait(barrier, 1 + 15 + 7)

    quarter = lax.broadcasted_iota(jnp.int32, (16, 128), 1) // 32

    def top_xy(some):
        for d in some:
            i = xy_of(TOP) + flip(d)
            cr(TOP, i).wait_recv()
            at = place(TOP, core, i)
            part[at] = part[at] + core_in[core_slot(TOP) + i]
            xr(TOP, d).start()

    def top_sum():
        i = xy_of(TOP)
        cr(TOP, i).wait_recv()
        total = part[mine(TOP)] + core_in[core_slot(TOP) + i]
        for d in range(1, 16):
            xr(TOP, d).wait_recv()
            total = total + xy_in[xy_slot(TOP) + d - 1]
        z_out[TOP] = total

    def top_rows():
        for d in range(1, SEPS):
            zr(TOP, d).wait_recv()

    C, D = 0, 1
    for v in range(TOP):
        if v >= 1:
            n = 2 ** (v - 1)
            step = min(n, 4)

            def theirs(i, carry):
                for j in range(step):
                    couple_chunk(v, xs, other, i * step + j)
                    cr(v, i * step + j).start()
                return carry

            def ours(i, carry):
                for j in range(step):
                    couple_chunk(v, xs, core, i * step + j)
                return carry

            if n == step:
                theirs(0, 0)
                ours(0, 0)
            else:
                lax.fori_loop(0, n // step, theirs, 0)
                lax.fori_loop(0, n // step, ours, 0)
            for d in peers(v):
                i = xy_of(v) + flip(d)
                cr(v, i).wait_recv()
                at = place(v, core, i)
                part[at] = part[at] + core_in[core_slot(v) + i]
                xr(v, d).start()
            fire({2: ((C, 2), (C, 6)), 3: ((C, 3), (C, 5)), 4: ((D, 3), (D, 5))}.get(v, ()))
            i = xy_of(v)
            cr(v, i).wait_recv()
            total = part[mine(v)] + core_in[core_slot(v) + i]
            for d in peers(v):
                xr(v, d).wait_recv()
                total = total + xy_in[xy_slot(v) + d - 1]
            z_out[v] = total
        for d in range(1, SEPS):
            zr(v, d).start()
        if v == 0:
            prep(0)
            terms(1)
            prep(1)
            terms(2)
        elif v == 1:
            load_c(TOP).wait()
            load_d(TOP).wait()
            fire(((C, 1), (C, 7)))
            prep(2)
            top_terms()
            for i in range(2 ** (TOP - 1)):
                cr(TOP, i).start()
        elif v == 2:
            prep(3)
            top_xy(range(8, 16))
        elif v == 3:
            prep(4)
            top_sum()
        else:
            wide_prep(C)
        if v >= 1:
            for i in range(2 ** (v - 1)):
                cr(v, i).wait_send()
            for d in peers(v):
                xr(v, d).wait_send()
        total = z_out[v, sep]
        for d in range(1, SEPS):
            zr(v, d).wait_recv()
            total = total + z_in[v, d - 1]
        resid[mine(v), sep] = total
        for d in range(1, SEPS):
            zg(v, d).start()
        if v == 0:
            terms(3)
        elif v == 1:
            fire(((D, 1), (D, 7)))
            terms(4)
            top_xy(range(1, 8))
        elif v == 4:
            top_rows()
        for d in range(1, SEPS):
            zr(v, d).wait_send()
        for d in range(1, SEPS):
            zg_in(v, d).wait_recv()
        if v >= 1:
            cg(v, 0).start()
            for d in peers(v):
                xg(v, d).start()
        if v == 3:
            for d in range(1, SEPS):
                zr(TOP, d).start()
        fire({2: ((D, 2), (D, 6)), 3: ((C, 4),), 4: ((D, 4),)}.get(v, ()))
        acc = jnp.zeros((2 * RHS, 128), F32)
        if v == 0:
            acc = product(0, 0, 0, 0, acc)
        else:
            acc = product(v, core, xy_of(v), mine(v), acc)
            for d in peers(v):
                xg(v, d, True).wait_recv()
                cg(v, d).start()
                i = xy_of(v) + flip(d)
                acc = product(v, core, i, place(v, core, i), acc)
            for d in range(2 ** (v - 1)):
                cg(v, d, True).wait_recv()
                i = xy_of(v) + flip(d)
                acc = product(v, other, i, place(v, other, i), acc)
        t = acc[:RHS] + acc[RHS:]
        x = t + pltpu.roll(t, 32, 1)
        if v == TOP - 1:
            x_all[sep] = functools.reduce(
                lambda kept, b: jnp.where(quarter == b, x[16 * b : 16 * b + 16], kept),
                range(1, 4), x[:16])
            for d in range(1, SEPS):
                xa(d).start()
        if v < 4:
            old = jnp.zeros_like(x) if v == 0 else sep_out[:, :128]
            sep_out[:, :128] = jnp.where(lanes // 32 == v, x, old)
        else:
            sep_out[:, 32 * v : 32 * v + 32] = x[:, 32 * (v - 4) : 32 * (v - 3)]
        if v < TOP - 1:
            hi, lo = split(x)
            xs = jnp.where(lanes < 64, hi.astype(F32), lo.astype(F32)).astype(BF16)
        for d in range(1, SEPS):
            zg(v, d).wait_send()
        if v >= 1:
            for d in range(2 ** (v - 1)):
                cg(v, d).wait_send()
            for d in peers(v):
                xg(v, d).wait_send()

    for d in range(1, SEPS):
        xa(d, True).wait_recv()

    def merged(pieces):
        return functools.reduce(
            lambda kept, b: jnp.where(quarter == b, pieces[b], kept), range(1, 4), pieces[0])

    def turned(tile, quarters):
        shift = 32 * (quarters % 4)
        return pltpu.roll(tile, shift, 1) if shift else tile

    below = [x_all[s] for s in range(SEPS)]
    x = jnp.concatenate([
        jnp.concatenate([merged([turned(below[4 * h + q], q - b) for q in range(4)])
                         for b in range(4)], axis=0)
        for h in range(2)], axis=1)
    hi, lo = split(x)
    both = jnp.concatenate([hi, lo], axis=0)
    for j in range(TOP_CHUNKS):
        cols = slice(j * CH, j * CH + CH)
        t = jnp.dot(both, wide_hi[C, :, cols], preferred_element_type=F32)
        t = t[:RHS] + t[RHS:] + jnp.dot(hi, wide_lo[C, :, cols], preferred_element_type=F32)
        for g in range(8):
            tiles[g % 2, j * 4 + g // 2] = -t[8 * g : 8 * g + 8]
    uc().start()
    wide_prep(D)
    uc().wait_recv()
    for d in range(1, 16):
        at = xy_of(TOP) + flip(d)
        tiles[core, at] = tiles[core, at] + tiles_core[at]
        ux(d).start()
    at = xy_of(TOP)
    total = z_out[TOP, sep] + (tiles[core, at] + tiles_core[at])
    for d in range(1, SEPS):
        total = total + z_in[TOP, d - 1]
    for d in range(1, 16):
        ux(d).wait_recv()
        total = total + tiles_xy[d - 1]
    tiles_res[core, at] = total
    tc(0).start()
    for d in range(1, 16):
        tg(d).start()
    for d in range(1, 16):
        tg(d, True).wait_recv()
        tc(d).start()
    for d in range(16):
        tc(d, True).wait_recv()
    solved_top = jnp.zeros((RHS, CH), F32)
    dims = (((1,), (1,)), ((), ()))
    for j in range(TOP_CHUNKS):
        cols = slice(j * CH, j * CH + CH)
        hi, lo = split(jnp.concatenate([tiles_res[g % 2, j * 4 + g // 2] for g in range(8)], axis=0))
        both = jnp.concatenate([hi, lo], axis=0)
        t = lax.dot_general(both, wide_hi[D, :, cols], dims, preferred_element_type=F32)
        solved_top = solved_top + t[:RHS] + t[RHS:] + lax.dot_general(
            hi, wide_lo[D, :, cols], dims, preferred_element_type=F32)
    for h in range(2):
        rows = [solved_top[16 * b : 16 * b + 16, 128 * h : 128 * h + 128] for b in range(4)]
        for q in range(4):
            x_out[4 * h + q] = merged([turned(rows[b], b - q) for b in range(4)])
    for d in range(1, SEPS):
        xo(d).start()
    for d in range(1, SEPS):
        xa(d).wait_send()
        wide(C, d).wait_send()
        wide(D, d).wait_send()
        zr(TOP, d).wait_send()
    for i in range(2 ** (TOP - 1)):
        cr(TOP, i).wait_send()
        tc(i).wait_send()
    uc().wait_send()
    for d in range(1, 16):
        xr(TOP, d).wait_send()
        ux(d).wait_send()
        tg(d).wait_send()
    total = x_out[sep]
    for d in range(1, SEPS):
        xo(d).wait_recv()
        total = total + x_in[d - 1]
    for b in range(4):
        sep_out[16 * b : 16 * b + 16, 32 * TOP : 32 * TOP + 32] = turned(total, 1 - b)[:, 32:64]
    for d in range(1, SEPS):
        xo(d).wait_send()


def body(
    leaf_rhs, leaf_inv, leaf_coupling, block_mask, leaf_rows, sep_rhs, dinv_rows, sep_coupling
):
    sums = leaf_coupling.shape[3]
    parents = sep_coupling.shape[3]
    dma = pltpu.SemaphoreType.DMA
    vmem = pl.BlockSpec(memory_space=pltpu.VMEM)
    smem = pl.BlockSpec(memory_space=pltpu.SMEM)
    hbm = pl.BlockSpec(memory_space=pl.ANY)
    leaf_solution, sep_solution = pl.pallas_call(
        kernel,
        out_shape=(
            jax.ShapeDtypeStruct((RHS, CH), BF16),
            jax.ShapeDtypeStruct((RHS, LEVELS * 32), F32),
        ),
        in_specs=[smem, smem, vmem, vmem, vmem, hbm, hbm, hbm],
        out_specs=(vmem, vmem),
        scratch_shapes=[
            pltpu.VMEM((CH, sums), BF16),
            pltpu.VMEM((32, sums), F32),
            pltpu.VMEM((32, parents), F32),
            pltpu.VMEM((128, sums), BF16),
            pltpu.VMEM((128, parents), BF16),
            pltpu.VMEM((63, SEPS, 8, CH), F32),
            pltpu.VMEM((31, SEPS, 8, CH), F32),
            pltpu.VMEM((26, SEPS, 8, CH), F32),
            pltpu.VMEM((LEVELS, SEPS, 8, CH), F32),
            pltpu.VMEM((LEVELS, SEPS - 1, 8, CH), F32),
            pltpu.VMEM((63, SEPS, 8, CH), F32),
            pltpu.VMEM((RHS, CH), BF16),
            pltpu.VMEM((2, SEPS, 32, TOP_CHUNKS * CH), F32),
            pltpu.VMEM((2, CH, TOP_CHUNKS * CH), BF16),
            pltpu.VMEM((2, CH, TOP_CHUNKS * CH), BF16),
            pltpu.VMEM((SEPS, 16, 128), F32),
            pltpu.VMEM((2, 16, 8, CH), F32),
            pltpu.VMEM((16, 8, CH), F32),
            pltpu.VMEM((15, 8, CH), F32),
            pltpu.VMEM((2, 16, 8, CH), F32),
            pltpu.VMEM((SEPS, 16, 128), F32),
            pltpu.VMEM((SEPS - 1, 16, 128), F32),
            dma((LEVELS,)), dma((LEVELS,)), dma((LEVELS,)),
            dma((LEVELS, 7)), dma((LEVELS, 7)), dma((LEVELS, 7)), dma((LEVELS, 7)),
            dma((26,)), dma((26,)), dma((26,)), dma((26,)),
            dma((31,)), dma((31,)), dma((31,)), dma((31,)),
            dma((2, 7)), dma((2, 7)), dma((7,)), dma((7,)), dma((1,)), dma((1,)),
            dma((15,)), dma((15,)), dma((15,)), dma((15,)), dma((16,)), dma((16,)),
            dma((7,)), dma((7,)),
        ],
        compiler_params=pltpu.CompilerParams(
            collective_id=0, has_side_effects=True, vmem_limit_bytes=60 * 2**20),
        name="forward_substitution",
    )(
        block_mask[0, 0], leaf_rows, leaf_rhs[:, 0, 0, :], leaf_inv[0, 0], sep_rhs[:, 0, 0, :],
        leaf_coupling[0, 0], dinv_rows[0, 0], sep_coupling[0, 0],
    )
    return (leaf_solution[:, None, None, :], sep_solution[:, None, None, :])


def solution(mesh):
    return jax.shard_map(
        body,
        mesh=mesh,
        in_specs=(
            P(None, "leaf", "sep", None),
            P("leaf", "sep", None, None),
            P("leaf", "sep", None, None),
            P("leaf", "sep", None),
            P("leaf", "sep"),
            P(None, "leaf", "sep", None),
            P("leaf", "sep", None, None),
            P("leaf", "sep", None, None),
        ),
        out_specs=(P(None, "leaf", "sep", None), P(None, "leaf", "sep", None)),
        check_vma=False,
    )
```

```python
import functools

import jax
import jax.numpy as jnp
from jax import lax
from jax.experimental import pallas as pl
from jax.experimental.pallas import tpu as pltpu
from jax.sharding import PartitionSpec as P

MESH = pl.DeviceIdType.MESH
LEVELS = 6
TOP = LEVELS - 1
TOP_CHUNKS = 4
ORDER = (4, 3, 5, 2, 6, 1, 7, 0)
W_PARTS = (0, 1, 3, 5, 6)
D_PARTS = (0, 2, 5, 6)
GROUPS = ((0, 3), (3, 2), (5, 3))
SEPS = 8
RHS = 64
CH = 256
F32 = jnp.float32
BF16 = jnp.bfloat16


def first_chunk(v):
    return 2**v - 1


def xy_slot(v):
    return sum(2 ** (u - 1) - 1 for u in range(2, v))


def core_slot(v):
    return 2 ** (v - 1) - 1


def split(x):
    hi = x.astype(BF16)
    lo = (x - hi.astype(F32)).astype(BF16)
    return hi, lo


def kernel(
    mask_ref, rows_ref, rhs_ref, inv_ref, srhs_ref, coup_hbm, dinv_hbm, scoup_hbm,
    leaf_out, sep_out,
    weights, dfull, cfull, dstack, cstack, part, core_in, xy_in, z_out, z_in, resid, sol_ref,
    turn_a, turn_b, sol_rel, srhs_rel, sep_rel,
    wide_in, wide_hi, wide_lo, x_all, tiles, tiles_core, tiles_xy, tiles_res, x_out, x_in,
    sem_w, sem_d, sem_c, send, z_sem, core_sem, xr_sem, xg_sem, top_sem,
):
    leaf = lax.axis_index("leaf")
    sep = lax.axis_index("sep")
    core = lax.rem(leaf, 2)
    other = 1 - core
    bits = [lax.rem(leaf // 2 ** (k + 1), 2) for k in range(4)]
    partner = leaf + 1 - 2 * core

    def xy_of(v):
        return lax.rem(leaf // 2, 2 ** (v - 1))

    def flip(d):
        return sum(2**k * (1 - 2 * bits[k]) for k in range(4) if d >> k & 1)

    def place(v, which_core, xy):
        if v == 0:
            return 0
        return first_chunk(v) + which_core * 2 ** (v - 1) + xy

    def mine(v):
        return 0 if v == 0 else place(v, core, xy_of(v))

    def column(v, which_core, xy):
        if v == 0:
            return 0
        return pl.multiple_of((first_chunk(v) + 2 * xy + which_core) * CH, CH)

    def peers(v):
        return range(1, 2 ** (v - 1)) if v >= 2 else range(0)

    def load_w(k):
        cols = pl.ds(first_chunk(W_PARTS[k]) * CH,
                     (first_chunk(W_PARTS[k + 1]) - first_chunk(W_PARTS[k])) * CH)
        return pltpu.make_async_copy(coup_hbm.at[:, cols], weights.at[:, cols], sem_w.at[k])

    def load_d(k):
        cols = pl.ds(first_chunk(D_PARTS[k]) * CH,
                     (first_chunk(D_PARTS[k + 1]) - first_chunk(D_PARTS[k])) * CH)
        return pltpu.make_async_copy(dinv_hbm.at[:, cols], dfull.at[:, cols], sem_d.at[k])

    def load_c(k):
        start = max(first_chunk(D_PARTS[k]) - 1, 0)
        cols = pl.ds(start * CH, (first_chunk(D_PARTS[k + 1]) - 1 - start) * CH)
        return pltpu.make_async_copy(scoup_hbm.at[:, cols], cfull.at[:, cols], sem_c.at[k])

    def remote(src, dst, sent, arrived, to):
        return pltpu.make_async_remote_copy(
            src_ref=src, dst_ref=dst, send_sem=sent, recv_sem=arrived,
            device_id=to, device_id_type=MESH)

    def z_peer(d):
        return lax.rem(sep + d, SEPS)

    next_z = (leaf, z_peer(1))
    next_core = (partner, sep)
    next_xy = (leaf + 2 * flip(1), sep)

    def zr(v, d):
        top = v == TOP
        return remote(z_out.at[v, z_peer(d) if top else ORDER.index(d)], z_in.at[v, d - 1],
                      send.at[1 if top else 0], top_sem.at[0] if top else z_sem.at[0],
                      (leaf, z_peer(d)))

    def all_zr(v):
        top = v == TOP
        return remote(z_in.at[v], z_in.at[v], send.at[1 if top else 0],
                      top_sem.at[0] if top else z_sem.at[0], next_z)

    def zg(v, d):
        there = ORDER.index(SEPS - d)
        g = [first <= there < first + count for first, count in GROUPS].index(True)
        return remote(resid.at[mine(v), SEPS - 1], resid.at[mine(v), there],
                      send.at[2], z_sem.at[1 + g], (leaf, z_peer(d)))

    def all_zg(v, g):
        first, count = GROUPS[g]
        rows = resid.at[mine(v), pl.ds(first, count - (g == 2))]
        return remote(rows, rows, send.at[2], z_sem.at[1 + g], next_z)

    def all_zg_sent(v):
        return remote(z_in.at[v], z_in.at[v], send.at[2], z_sem.at[1], next_z)

    def rows_of(g):
        return pl.ds(*GROUPS[g])

    def xr(v, d, g):
        k = xy_slot(v) + d - 1
        at = place(v, core, xy_of(v) + flip(d))
        to = (leaf + 2 * flip(d), sep)
        if v == TOP:
            return remote(part.at[at], xy_in.at[k], send.at[4], top_sem.at[1], to)
        return remote(part.at[at, rows_of(g)], xy_in.at[k, rows_of(g)],
                      send.at[3], xr_sem.at[v - 2, g], to)

    def all_xr(v, g):
        slots = pl.ds(xy_slot(v), len(peers(v)))
        if v == TOP:
            ref = xy_in.at[slots]
            return remote(ref, ref, send.at[4], top_sem.at[1], next_xy)
        ref = xy_in.at[slots, rows_of(g)]
        return remote(ref, ref, send.at[3], xr_sem.at[v - 2, g], next_xy)

    def all_xr_sent(v):
        ref = xy_in.at[pl.ds(xy_slot(v), len(peers(v)))]
        return remote(ref, ref, send.at[3], xr_sem.at[v - 2, 0], next_xy)

    def xg(v, d, g):
        at = mine(v)
        return remote(resid.at[at, rows_of(g)], resid.at[at, rows_of(g)],
                      send.at[5], xg_sem.at[d - 1], (leaf + 2 * flip(d), sep))

    def all_xg(v, d):
        ref = resid.at[place(v, core, xy_of(v) + flip(d))]
        return remote(ref, ref, send.at[5], xg_sem.at[d - 1], (leaf + 2 * flip(d), sep))

    def all_xg_sent(v):
        ref = xy_in.at[pl.ds(xy_slot(v), len(peers(v)))]
        return remote(ref, ref, send.at[5], xg_sem.at[0], next_xy)

    def cr(v, i):
        top = v == TOP
        return remote(part.at[place(v, other, i)], core_in.at[core_slot(v) + i],
                      send.at[7 if top else 6], top_sem.at[2] if top else core_sem.at[0],
                      next_core)

    def all_cr(v):
        top = v == TOP
        ref = core_in.at[pl.ds(core_slot(v), 2 ** (v - 1))]
        return remote(ref, ref, send.at[7 if top else 6],
                      top_sem.at[2] if top else core_sem.at[0], next_core)

    def cg(v, d):
        ref = resid.at[place(v, core, xy_of(v) + flip(d))]
        return remote(ref, ref, send.at[8], core_sem.at[1], next_core)

    def all_cg(v):
        ref = resid.at[pl.ds(place(v, other, 0), 2 ** (v - 1))]
        return remote(ref, ref, send.at[8], core_sem.at[1], next_core)

    def wide(a, d):
        src, first = ((cfull, first_chunk(TOP) - 1), (dfull, first_chunk(TOP)))[a]
        to = z_peer(d)
        cols = pl.ds(pl.multiple_of((first + to * TOP_CHUNKS) * CH, CH), TOP_CHUNKS * CH)
        return remote(src.at[:, cols], wide_in.at[a, d - 1],
                      send.at[9], top_sem.at[3 + a], (leaf, to))

    def all_wide(a):
        return remote(wide_in.at[a], wide_in.at[a], send.at[9], top_sem.at[3 + a], next_z)

    def fire(pieces):
        for a, d in pieces:
            wide(a, d).start()

    def wide_stack(a, at, block):
        rows = pl.ds(pl.multiple_of(at * 32, 32), 32)
        hi, lo = split(block)
        wide_hi[a, rows, :] = hi
        wide_lo[a, rows, :] = lo

    def wide_prep(a):
        src, first = ((cfull, first_chunk(TOP) - 1), (dfull, first_chunk(TOP)))[a]
        cols = pl.ds(pl.multiple_of((first + sep * TOP_CHUNKS) * CH, CH), TOP_CHUNKS * CH)
        wide_stack(a, sep, src[:, cols])
        all_wide(a).wait_recv()
        for d in range(1, SEPS):
            wide_stack(a, z_peer(SEPS - d), wide_in[a, d - 1])

    def xa(d):
        return remote(x_all.at[0], x_all.at[d], send.at[10], top_sem.at[5], (leaf, z_peer(d)))

    def all_xa():
        ref = x_all.at[pl.ds(1, SEPS - 1)]
        return remote(ref, ref, send.at[10], top_sem.at[5], next_z)

    def uc():
        return remote(tiles.at[other], tiles_core, send.at[11], top_sem.at[6], next_core)

    def ux(d):
        return remote(tiles.at[core, xy_of(TOP) + flip(d)], tiles_xy.at[d - 1],
                      send.at[12], top_sem.at[7], (leaf + 2 * flip(d), sep))

    def all_ux():
        return remote(tiles_xy, tiles_xy, send.at[12], top_sem.at[7], next_xy)

    def tg(d):
        return remote(tiles_res.at[0, 0], tiles_res.at[0, d],
                      send.at[13], top_sem.at[8], (leaf + 2 * flip(d), sep))

    def all_tg():
        ref = tiles_res.at[0, pl.ds(1, 15)]
        return remote(ref, ref, send.at[13], top_sem.at[8], next_xy)

    def tc():
        return remote(tiles_res.at[0], tiles_res.at[1], send.at[14], top_sem.at[9], next_core)

    def xo(d):
        return remote(x_out.at[z_peer(d)], x_in.at[d - 1], send.at[15], top_sem.at[10],
                      (leaf, z_peer(d)))

    def all_xo():
        return remote(x_in, x_in, send.at[15], top_sem.at[10], next_z)

    barrier = pltpu.get_barrier_semaphore()
    pl.semaphore_signal(barrier, inc=1, device_id=(partner, sep), device_id_type=MESH)
    for d in range(1, 16):
        pl.semaphore_signal(
            barrier, inc=1, device_id=(leaf + 2 * flip(d), sep), device_id_type=MESH)
    for d in range(1, SEPS):
        pl.semaphore_signal(
            barrier, inc=1, device_id=(leaf, z_peer(d)), device_id_type=MESH)

    load_w(0).start()
    load_d(0).start()
    load_c(0).start()
    load_w(1).start()
    load_d(1).start()
    load_c(1).start()
    load_w(2).start()
    load_d(2).start()
    load_c(2).start()
    load_w(3).start()

    live = lax.broadcasted_iota(jnp.int32, (RHS, CH), 1) < rows_ref[0, 0]
    right = jnp.where(live, rhs_ref[...].astype(F32), 0.0).astype(BF16)
    solved = jnp.dot(right, inv_ref[...], preferred_element_type=F32)
    solved = jnp.where(live, solved, 0.0)
    sol_ref[...] = solved.astype(BF16)
    leaf_out[...] = solved.astype(BF16)

    def turned_rows(scratch, value):
        scratch[...] = value.reshape(scratch.shape)
        return jnp.concatenate([scratch[z_peer(d)] for d in ORDER], axis=0)

    sol_rel[...] = turned_rows(turn_a, solved).astype(BF16)
    srhs_rel[...] = turned_rows(turn_b, srhs_ref[...].astype(F32)).astype(BF16)

    def terms_chunk(v, which_core, xy):
        m = 0 if v == 0 else 2 * xy + which_core
        block = 2 * (first_chunk(v) + m)
        col = column(v, which_core, xy)
        t = jnp.dot(sol_rel[...], weights[:, pl.ds(col, CH)], preferred_element_type=F32)
        left = t[:, :128] * (-mask_ref[block].astype(F32))
        rest = t[:, 128:] * (-mask_ref[block + 1].astype(F32))
        t = jnp.concatenate([left, rest], axis=1)
        part[place(v, which_core, xy)] = t.reshape(SEPS, 8, CH)

    def own_rows(v, rows_ref):
        r = lax.broadcasted_iota(jnp.int32, (LEVELS * 32, CH), 0)
        c = lax.broadcasted_iota(jnp.int32, (LEVELS * 32, CH), 1)
        pick = jnp.where((r - 32 * v == c - 32 * sep) & (r >= 32 * v) & (r < 32 * v + 32), 1.0, 0.0)
        own = jnp.dot(rows_ref[...], pick.astype(BF16), preferred_element_type=F32)
        return own.reshape(SEPS, 8, CH)

    def tile_place(j, g):
        return first_chunk(TOP) + (g % 2) * 2 ** (TOP - 1) + j * 4 + g // 2

    def top_terms():
        def some(at, carry):
            for j in range(TOP_CHUNKS):
                m = at * TOP_CHUNKS + j
                block = 2 * (first_chunk(TOP) + m)
                col = pl.multiple_of((first_chunk(TOP) + m) * CH, CH)
                t = jnp.dot(sol_ref[...], weights[:, pl.ds(col, CH)], preferred_element_type=F32)
                left = t[:, :128] * (-mask_ref[block].astype(F32))
                rest = t[:, 128:] * (-mask_ref[block + 1].astype(F32))
                t = jnp.concatenate([left, rest], axis=1)
                for g in range(8):
                    part[tile_place(j, g), at] = t[8 * g : 8 * g + 8]
            return carry

        lax.fori_loop(0, SEPS, some, 0)
        own = own_rows(TOP, srhs_ref)
        at = leaf // TOP_CHUNKS
        j = lax.rem(leaf, TOP_CHUNKS)
        for g in range(8):
            k = tile_place(j, g)
            part[k, at] = part[k, at] + own[g]

    def terms(v):
        if v == 0:
            terms_chunk(0, 0, 0)
        else:
            n = 2 ** (v - 1)
            step = min(n, 2)

            def some(i, carry):
                for j in range(step):
                    for c in range(2):
                        terms_chunk(v, c, i * step + j)
                return carry

            if n == step:
                some(0, 0)
            else:
                lax.fori_loop(0, n // step, some, 0)
        at = mine(v)
        part[at] = part[at] + own_rows(v, srhs_rel)

    def stack(src, dst, start, size):
        cols = pl.ds(pl.multiple_of(start, CH), size)
        hi, lo = split(src[:, cols])
        dst[0:32, cols] = hi
        dst[32:64, cols] = lo
        dst[64:96, cols] = hi
        dst[96:128, cols] = lo

    def stack_all(src, dst, start, size):
        width = min(size, 512)
        if size == width:
            stack(src, dst, start, size)
        else:
            def some(i, carry):
                stack(src, dst, start + i * width, width)
                return carry
            lax.fori_loop(0, size // width, some, 0)

    def prep(v):
        stack_all(dfull, dstack, first_chunk(v) * CH, 2**v * CH)
        if v:
            stack_all(cfull, cstack, (first_chunk(v) - 1) * CH, 2**v * CH)

    lanes = lax.broadcasted_iota(jnp.int32, (RHS, 128), 1)

    def product(v, which_core, xy, at, acc):
        hi, lo = split(resid[at].reshape(RHS, CH))
        rows = jnp.concatenate([hi, lo], axis=0)
        col = column(v, which_core, xy)
        return acc + lax.dot_general(
            rows, dstack[:, pl.ds(col, CH)], (((1,), (1,)), ((), ())),
            preferred_element_type=F32)

    def couple_chunk(v, xs, which_core, xy):
        at = place(v, which_core, xy)
        col = (first_chunk(v) - 1 + 2 * xy + which_core) * CH
        t = jnp.dot(xs, cstack[:, pl.ds(pl.multiple_of(col, CH), CH)], preferred_element_type=F32)
        part[at] = part[at] - t.reshape(SEPS, 8, CH)

    load_w(0).wait()
    terms(0)
    z_out[0] = part[0]
    pl.semaphore_wait(barrier, 1 + 15 + 7)

    quarter = lax.broadcasted_iota(jnp.int32, (16, 128), 1) // 32

    def top_xy(some):
        for d in some:
            i = xy_of(TOP) + flip(d)
            at = place(TOP, core, i)
            part[at] = part[at] + core_in[core_slot(TOP) + i]
            xr(TOP, d, None).start()

    def top_sum():
        i = xy_of(TOP)
        all_xr(TOP, None).wait_recv()
        total = part[mine(TOP)] + core_in[core_slot(TOP) + i]
        for d in range(1, 16):
            total = total + xy_in[xy_slot(TOP) + d - 1]
        z_out[TOP] = total

    C, D = 0, 1
    for v in range(TOP):
        if v >= 1:
            n = 2 ** (v - 1)
            step = min(n, 4)

            def theirs(i, carry):
                for j in range(step):
                    couple_chunk(v, xs, other, i * step + j)
                    cr(v, i * step + j).start()
                return carry

            def ours(i, carry):
                for j in range(step):
                    couple_chunk(v, xs, core, i * step + j)
                return carry

            if n == step:
                theirs(0, 0)
                ours(0, 0)
            else:
                lax.fori_loop(0, n // step, theirs, 0)
                lax.fori_loop(0, n // step, ours, 0)
            all_cr(v).wait_recv()
            for d in peers(v):
                i = xy_of(v) + flip(d)
                at = place(v, core, i)
                part[at] = part[at] + core_in[core_slot(v) + i]
                xr(v, d, 0).start()
            for g in range(1, 3):
                for d in peers(v):
                    xr(v, d, g).start()
            fire({2: ((C, 2), (C, 6)), 3: ((C, 3), (C, 5)), 4: ((D, 3), (D, 5))}.get(v, ()))
            i = xy_of(v)
            at = mine(v)
            part[at] = part[at] + core_in[core_slot(v) + i]
            for g, (first, count) in enumerate(GROUPS):
                total = part[at, first : first + count]
                if v >= 2:
                    all_xr(v, g).wait_recv()
                for d in peers(v):
                    total = total + xy_in[xy_slot(v) + d - 1, first : first + count]
                z_out[v, first : first + count] = total
                for d in ORDER[first : first + count]:
                    if d:
                        zr(v, d).start()
        else:
            for d in range(1, SEPS):
                zr(v, d).start()
        if v == 0:
            load_d(0).wait()
            load_c(0).wait()
            prep(0)
            load_w(1).wait()
            terms(1)
            prep(1)
            terms(2)
        elif v == 1:
            load_c(2).wait()
            load_d(2).wait()
            fire(((C, 1), (C, 7)))
            load_d(1).wait()
            load_c(1).wait()
            prep(2)
            load_w(3).wait()
            top_terms()
            for i in range(2 ** (TOP - 1)):
                cr(TOP, i).start()
        elif v == 2:
            prep(3)
            top_xy(range(8, 16))
        elif v == 3:
            prep(4)
            top_sum()
        else:
            wide_prep(C)
        if v >= 1:
            all_cr(v).wait_send()
            if v >= 2:
                all_xr_sent(v).wait_send()
        total = z_out[v, SEPS - 1]
        all_zr(v).wait_recv()
        for d in range(1, SEPS):
            total = total + z_in[v, d - 1]
        resid[mine(v), SEPS - 1] = total
        for d in range(1, SEPS):
            zg(v, d).start()
        if v == 0:
            load_w(2).wait()
            terms(3)
        elif v == 1:
            fire(((D, 1), (D, 7)))
            terms(4)
            all_cr(TOP).wait_recv()
            top_xy(range(1, 8))
        elif v == 4:
            all_zr(TOP).wait_recv()
        all_zr(v).wait_send()
        for g, (first, count) in reversed(list(enumerate(GROUPS))):
            all_zg(v, g).wait_recv()
            for d in peers(v):
                xg(v, d, g).start()
        if v >= 1:
            cg(v, 0).start()
        if v == 3:
            for d in range(1, SEPS):
                zr(TOP, d).start()
        fire({2: ((D, 2), (D, 6)), 3: ((C, 4),), 4: ((D, 4),)}.get(v, ()))
        acc = jnp.zeros((2 * RHS, 128), F32)
        if v == 0:
            acc = product(0, 0, 0, 0, acc)
        else:
            acc = product(v, core, xy_of(v), mine(v), acc)
            for d in peers(v):
                all_xg(v, d).wait_recv()
                cg(v, d).start()
                i = xy_of(v) + flip(d)
                acc = product(v, core, i, place(v, core, i), acc)
            all_cg(v).wait_recv()
            for d in range(2 ** (v - 1)):
                i = xy_of(v) + flip(d)
                acc = product(v, other, i, place(v, other, i), acc)
        t = acc[:RHS] + acc[RHS:]
        x = t + pltpu.roll(t, 32, 1)
        if v == TOP - 1:
            for p, d in enumerate(ORDER):
                turn_a[z_peer(d), :, :128] = x[8 * p : 8 * p + 8]
            x = turn_a[:, :, :128].reshape(RHS, 128)
            x_all[0] = functools.reduce(
                lambda kept, b: jnp.where(quarter == b, x[16 * b : 16 * b + 16], kept),
                range(1, 4), x[:16])
            for d in range(1, SEPS):
                xa(d).start()
        if v < 4:
            old = jnp.zeros_like(x) if v == 0 else sep_rel[...]
            sep_rel[...] = jnp.where(lanes // 32 == v, x, old)
        else:
            sep_out[:, 32 * v : 32 * v + 32] = x[:, 32 * (v - 4) : 32 * (v - 3)]
        if v < TOP - 1:
            hi, lo = split(x)
            xs = jnp.where(lanes < 64, hi.astype(F32), lo.astype(F32)).astype(BF16)
        all_zg_sent(v).wait_send()
        if v >= 1:
            all_cg(v).wait_send()
        if v >= 2:
            all_xg_sent(v).wait_send()

    for p, d in enumerate(ORDER):
        rows = pl.ds(pl.multiple_of(8 * z_peer(d), 8), 8)
        sep_out[rows, :128] = sep_rel[8 * p : 8 * p + 8]

    all_xa().wait_recv()

    def merged(pieces):
        return functools.reduce(
            lambda kept, b: jnp.where(quarter == b, pieces[b], kept), range(1, 4), pieces[0])

    def turned(tile, quarters):
        shift = 32 * (quarters % 4)
        return pltpu.roll(tile, shift, 1) if shift else tile

    below = [x_all[lax.rem(sep + SEPS - s, SEPS)] for s in range(SEPS)]
    x = jnp.concatenate([
        jnp.concatenate([merged([turned(below[4 * h + q], q - b) for q in range(4)])
                         for b in range(4)], axis=0)
        for h in range(2)], axis=1)
    hi, lo = split(x)
    both = jnp.concatenate([hi, lo], axis=0)
    for j in range(TOP_CHUNKS):
        cols = slice(j * CH, j * CH + CH)
        t = jnp.dot(both, wide_hi[C, :, cols], preferred_element_type=F32)
        t = t[:RHS] + t[RHS:] + jnp.dot(hi, wide_lo[C, :, cols], preferred_element_type=F32)
        for g in range(8):
            tiles[g % 2, j * 4 + g // 2] = -t[8 * g : 8 * g + 8]
    uc().start()
    wide_prep(D)
    uc().wait_recv()
    for d in range(1, 16):
        at = xy_of(TOP) + flip(d)
        tiles[core, at] = tiles[core, at] + tiles_core[at]
        ux(d).start()
    at = xy_of(TOP)
    total = z_out[TOP, sep] + (tiles[core, at] + tiles_core[at])
    for d in range(1, SEPS):
        total = total + z_in[TOP, d - 1]
    all_ux().wait_recv()
    for d in range(1, 16):
        total = total + tiles_xy[d - 1]
    tiles_res[0, 0] = total
    for d in range(1, 16):
        tg(d).start()
    all_tg().wait_recv()
    tc().start()
    tc().wait_recv()

    def tile(j, g):
        xy = j * 4 + g // 2
        slot = sum(2**k * (1 - bits[k] if xy >> k & 1 else bits[k]) for k in range(4))
        return tiles_res[other if g % 2 else core, slot]

    solved_top = jnp.zeros((RHS, CH), F32)
    dims = (((1,), (1,)), ((), ()))
    for j in range(TOP_CHUNKS):
        cols = slice(j * CH, j * CH + CH)
        hi, lo = split(jnp.concatenate([tile(j, g) for g in range(8)], axis=0))
        both = jnp.concatenate([hi, lo], axis=0)
        t = lax.dot_general(both, wide_hi[D, :, cols], dims, preferred_element_type=F32)
        solved_top = solved_top + t[:RHS] + t[RHS:] + lax.dot_general(
            hi, wide_lo[D, :, cols], dims, preferred_element_type=F32)
    for h in range(2):
        rows = [solved_top[16 * b : 16 * b + 16, 128 * h : 128 * h + 128] for b in range(4)]
        for q in range(4):
            x_out[4 * h + q] = merged([turned(rows[b], b - q) for b in range(4)])
    for d in range(1, SEPS):
        xo(d).start()
    all_xa().wait_send()
    all_wide(C).wait_send()
    all_wide(D).wait_send()
    all_zr(TOP).wait_send()
    all_cr(TOP).wait_send()
    all_xr(TOP, None).wait_send()
    uc().wait_send()
    all_ux().wait_send()
    all_tg().wait_send()
    tc().wait_send()
    all_xo().wait_recv()
    total = x_out[sep]
    for d in range(1, SEPS):
        total = total + x_in[d - 1]
    for b in range(4):
        sep_out[16 * b : 16 * b + 16, 32 * TOP : 32 * TOP + 32] = turned(total, 1 - b)[:, 32:64]
    all_xo().wait_send()


def body(
    leaf_rhs, leaf_inv, leaf_coupling, block_mask, leaf_rows, sep_rhs, dinv_rows, sep_coupling
):
    sums = leaf_coupling.shape[3]
    parents = sep_coupling.shape[3]
    dma = pltpu.SemaphoreType.DMA
    vmem = pl.BlockSpec(memory_space=pltpu.VMEM)
    smem = pl.BlockSpec(memory_space=pltpu.SMEM)
    hbm = pl.BlockSpec(memory_space=pl.ANY)
    leaf_solution, sep_solution = pl.pallas_call(
        kernel,
        out_shape=(
            jax.ShapeDtypeStruct((RHS, CH), BF16),
            jax.ShapeDtypeStruct((RHS, LEVELS * 32), F32),
        ),
        in_specs=[smem, smem, vmem, vmem, vmem, hbm, hbm, hbm],
        out_specs=(vmem, vmem),
        scratch_shapes=[
            pltpu.VMEM((CH, sums), BF16),
            pltpu.VMEM((32, sums), F32),
            pltpu.VMEM((32, parents), F32),
            pltpu.VMEM((128, sums), BF16),
            pltpu.VMEM((128, parents), BF16),
            pltpu.VMEM((63, SEPS, 8, CH), F32),
            pltpu.VMEM((31, SEPS, 8, CH), F32),
            pltpu.VMEM((26, SEPS, 8, CH), F32),
            pltpu.VMEM((LEVELS, SEPS, 8, CH), F32),
            pltpu.VMEM((LEVELS, SEPS - 1, 8, CH), F32),
            pltpu.VMEM((63, SEPS, 8, CH), F32),
            pltpu.VMEM((RHS, CH), BF16),
            pltpu.VMEM((SEPS, 8, CH), F32),
            pltpu.VMEM((SEPS, 8, LEVELS * 32), F32),
            pltpu.VMEM((RHS, CH), BF16),
            pltpu.VMEM((RHS, LEVELS * 32), BF16),
            pltpu.VMEM((RHS, 128), F32),
            pltpu.VMEM((2, SEPS - 1, 32, TOP_CHUNKS * CH), F32),
            pltpu.VMEM((2, CH, TOP_CHUNKS * CH), BF16),
            pltpu.VMEM((2, CH, TOP_CHUNKS * CH), BF16),
            pltpu.VMEM((SEPS, 16, 128), F32),
            pltpu.VMEM((2, 16, 8, CH), F32),
            pltpu.VMEM((16, 8, CH), F32),
            pltpu.VMEM((15, 8, CH), F32),
            pltpu.VMEM((2, 16, 8, CH), F32),
            pltpu.VMEM((SEPS, 16, 128), F32),
            pltpu.VMEM((SEPS - 1, 16, 128), F32),
            dma((4,)), dma((3,)), dma((3,)), dma((16,)), dma((4,)), dma((2,)), dma((3, 3)), dma((7,)),
            dma((11,)),
        ],
        compiler_params=pltpu.CompilerParams(
            collective_id=0, has_side_effects=True, vmem_limit_bytes=60 * 2**20),
        name="forward_substitution",
    )(
        block_mask[0, 0], leaf_rows, leaf_rhs[:, 0, 0, :], leaf_inv[0, 0], sep_rhs[:, 0, 0, :],
        leaf_coupling[0, 0], dinv_rows[0, 0], sep_coupling[0, 0],
    )
    return (leaf_solution[:, None, None, :], sep_solution[:, None, None, :])


def solution(mesh):
    return jax.shard_map(
        body,
        mesh=mesh,
        in_specs=(
            P(None, "leaf", "sep", None),
            P("leaf", "sep", None, None),
            P("leaf", "sep", None, None),
            P("leaf", "sep", None),
            P("leaf", "sep"),
            P(None, "leaf", "sep", None),
            P("leaf", "sep", None, None),
            P("leaf", "sep", None, None),
        ),
        out_specs=(P(None, "leaf", "sep", None), P(None, "leaf", "sep", None)),
        check_vma=False,
    )
```

```python
import functools

import jax
import jax.numpy as jnp
from jax import lax
from jax.experimental import pallas as pl
from jax.experimental.pallas import tpu as pltpu
from jax.sharding import PartitionSpec as P

MESH = pl.DeviceIdType.MESH
LEVELS = 6
SEPS = 8
TOP = LEVELS - 1
TOP_CHUNKS = 4
ORDER = (4, 3, 5, 2, 6, 1, 7, 0)
W_PARTS = (0, 1, 3, 5, 6)
D_PARTS = (0, 2, 5, 6)
C, D = 0, 1


def both_ways(a, d, *halves):
    return tuple((a, e, h) for h in halves or (0, 1) for e in sorted({d, SEPS - d}))


WIDE_COPIES = {
    (1, "z"): both_ways(C, 1),
    (1, "g"): both_ways(D, 1),
    (1, "x"): both_ways(C, 2),
    (2, "z"): both_ways(D, 2, 0),
    (2, "g"): both_ways(D, 2, 1),
    (2, "x"): both_ways(C, 3),
    (3, "z"): both_ways(D, 3, 0),
    (3, "g"): both_ways(D, 3, 1),
    (3, "x"): both_ways(C, 4),
    (4, "x"): both_ways(D, 4, 0),
    (5, "x"): both_ways(D, 4, 1),
}
GROUPS = ((0, 3), (3, 2), (5, 3))
RHS = 64
CH = 256
F32 = jnp.float32
BF16 = jnp.bfloat16


def first_chunk(v):
    return 2**v - 1


def xy_slot(v):
    return sum(2 ** (u - 1) - 1 for u in range(2, v))


def core_slot(v):
    return 2 ** (v - 1) - 1


def split(x):
    hi = x.astype(BF16)
    lo = (x - hi.astype(F32)).astype(BF16)
    return hi, lo


def kernel(
    mask_ref, rows_ref, rhs_hbm, inv_hbm, srhs_hbm, coup_hbm, dinv_hbm, scoup_hbm,
    leaf_out, sep_out,
    rhs_ref, inv_ref, srhs_ref,
    weights, dfull, cfull, dstack, cstack, part, core_in, xy_in, z_out, z_in, resid, sol_ref,
    turn_a, turn_b, sol_rel, srhs_rel, sep_rel,
    wide_in, wide_hi, wide_lo, x_all, tiles, tiles_core, tiles_xy, tiles_res, x_out, x_in,
    sem_in, sem_w, sem_d, sem_c, send, z_sem, core_sem, xr_sem, xg_sem, top_sem,
):
    leaf = lax.axis_index("leaf")
    sep = lax.axis_index("sep")
    core = lax.rem(leaf, 2)
    other = 1 - core
    bits = [lax.rem(leaf // 2 ** (k + 1), 2) for k in range(4)]
    partner = leaf + 1 - 2 * core

    def xy_of(v):
        return lax.rem(leaf // 2, 2 ** (v - 1))

    def flip(d):
        return sum(2**k * (1 - 2 * bits[k]) for k in range(4) if d >> k & 1)

    def place(v, which_core, xy):
        if v == 0:
            return 0
        return first_chunk(v) + which_core * 2 ** (v - 1) + xy

    def mine(v):
        return 0 if v == 0 else place(v, core, xy_of(v))

    def column(v, which_core, xy):
        if v == 0:
            return 0
        return pl.multiple_of((first_chunk(v) + 2 * xy + which_core) * CH, CH)

    def peers(v):
        return range(1, 2 ** (v - 1)) if v >= 2 else range(0)

    def load_w(k):
        cols = pl.ds(first_chunk(W_PARTS[k]) * CH,
                     (first_chunk(W_PARTS[k + 1]) - first_chunk(W_PARTS[k])) * CH)
        return pltpu.make_async_copy(coup_hbm.at[:, cols], weights.at[:, cols], sem_w.at[k])

    def load_d(k):
        cols = pl.ds(first_chunk(D_PARTS[k]) * CH,
                     (first_chunk(D_PARTS[k + 1]) - first_chunk(D_PARTS[k])) * CH)
        return pltpu.make_async_copy(dinv_hbm.at[:, cols], dfull.at[:, cols], sem_d.at[k])

    def load_c(k):
        start = max(first_chunk(D_PARTS[k]) - 1, 0)
        cols = pl.ds(start * CH, (first_chunk(D_PARTS[k + 1]) - 1 - start) * CH)
        return pltpu.make_async_copy(scoup_hbm.at[:, cols], cfull.at[:, cols], sem_c.at[k])

    def remote(src, dst, sent, arrived, to):
        return pltpu.make_async_remote_copy(
            src_ref=src, dst_ref=dst, send_sem=sent, recv_sem=arrived,
            device_id=to, device_id_type=MESH)

    def z_peer(d):
        return lax.rem(sep + d, SEPS)

    next_z = (leaf, z_peer(1))
    next_core = (partner, sep)
    next_xy = (leaf + 2 * flip(1), sep)

    def zr(v, d):
        top = v == TOP
        return remote(z_out.at[v, z_peer(d) if top else ORDER.index(d)], z_in.at[v, d - 1],
                      send.at[1 if top else 0], top_sem.at[0] if top else z_sem.at[0],
                      (leaf, z_peer(d)))

    def all_zr(v):
        top = v == TOP
        return remote(z_in.at[v], z_in.at[v], send.at[1 if top else 0],
                      top_sem.at[0] if top else z_sem.at[0], next_z)

    def zg(v, d):
        there = ORDER.index(SEPS - d)
        g = [first <= there < first + count for first, count in GROUPS].index(True)
        return remote(resid.at[mine(v), SEPS - 1], resid.at[mine(v), there],
                      send.at[2], z_sem.at[1 + g], (leaf, z_peer(d)))

    def all_zg(v, g):
        first, count = GROUPS[g]
        rows = resid.at[mine(v), pl.ds(first, count - (g == 2))]
        return remote(rows, rows, send.at[2], z_sem.at[1 + g], next_z)

    def all_zg_sent(v):
        return remote(z_in.at[v], z_in.at[v], send.at[2], z_sem.at[1], next_z)

    def rows_of(g):
        return pl.ds(*GROUPS[g])

    def xr(v, d, g):
        k = xy_slot(v) + d - 1
        at = place(v, core, xy_of(v) + flip(d))
        to = (leaf + 2 * flip(d), sep)
        if v == TOP:
            return remote(part.at[at], xy_in.at[k], send.at[4], top_sem.at[1], to)
        return remote(part.at[at, rows_of(g)], xy_in.at[k, rows_of(g)],
                      send.at[3], xr_sem.at[v - 2, g], to)

    def all_xr(v, g):
        slots = pl.ds(xy_slot(v), len(peers(v)))
        if v == TOP:
            ref = xy_in.at[slots]
            return remote(ref, ref, send.at[4], top_sem.at[1], next_xy)
        ref = xy_in.at[slots, rows_of(g)]
        return remote(ref, ref, send.at[3], xr_sem.at[v - 2, g], next_xy)

    def all_xr_sent(v):
        ref = xy_in.at[pl.ds(xy_slot(v), len(peers(v)))]
        return remote(ref, ref, send.at[3], xr_sem.at[v - 2, 0], next_xy)

    def xg(v, d, g):
        at = mine(v)
        return remote(resid.at[at, rows_of(g)], resid.at[at, rows_of(g)],
                      send.at[5], xg_sem.at[d - 1], (leaf + 2 * flip(d), sep))

    def all_xg(v, d):
        ref = resid.at[place(v, core, xy_of(v) + flip(d))]
        return remote(ref, ref, send.at[5], xg_sem.at[d - 1], (leaf + 2 * flip(d), sep))

    def all_xg_sent(v):
        ref = xy_in.at[pl.ds(xy_slot(v), len(peers(v)))]
        return remote(ref, ref, send.at[5], xg_sem.at[0], next_xy)

    def cr(v, i):
        top = v == TOP
        return remote(part.at[place(v, other, i)], core_in.at[core_slot(v) + i],
                      send.at[7 if top else 6], top_sem.at[2] if top else core_sem.at[0],
                      next_core)

    def all_cr(v):
        top = v == TOP
        ref = core_in.at[pl.ds(core_slot(v), 2 ** (v - 1))]
        return remote(ref, ref, send.at[7 if top else 6],
                      top_sem.at[2] if top else core_sem.at[0], next_core)

    def cg(v, d):
        ref = resid.at[place(v, core, xy_of(v) + flip(d))]
        return remote(ref, ref, send.at[8], core_sem.at[1], next_core)

    def all_cg(v):
        ref = resid.at[pl.ds(place(v, other, 0), 2 ** (v - 1))]
        return remote(ref, ref, send.at[8], core_sem.at[1], next_core)

    def wide(a, d, half):
        src, first = ((cfull, first_chunk(TOP) - 1), (dfull, first_chunk(TOP)))[a]
        to = z_peer(d)
        size = TOP_CHUNKS * CH // 2
        cols = pl.ds(pl.multiple_of((first + to * TOP_CHUNKS) * CH + half * size, CH), size)
        return remote(src.at[:, cols], wide_in.at[a, d - 1, :, pl.ds(half * size, size)],
                      send.at[9], top_sem.at[3 + a], (leaf, to))

    def all_wide(a):
        return remote(wide_in.at[a], wide_in.at[a], send.at[9], top_sem.at[3 + a], next_z)

    def fire(v, point):
        for piece in WIDE_COPIES.get((v, point), ()):
            wide(*piece).start()

    def wide_stack(a, at, block):
        rows = pl.ds(pl.multiple_of(at * 32, 32), 32)
        hi, lo = split(block)
        wide_hi[a, rows, :] = hi
        wide_lo[a, rows, :] = lo

    def wide_prep(a):
        src, first = ((cfull, first_chunk(TOP) - 1), (dfull, first_chunk(TOP)))[a]
        cols = pl.ds(pl.multiple_of((first + sep * TOP_CHUNKS) * CH, CH), TOP_CHUNKS * CH)
        wide_stack(a, sep, src[:, cols])
        all_wide(a).wait_recv()
        for d in range(1, SEPS):
            wide_stack(a, z_peer(SEPS - d), wide_in[a, d - 1])

    def xa(d):
        return remote(x_all.at[0], x_all.at[d], send.at[10], top_sem.at[5], (leaf, z_peer(d)))

    def all_xa():
        ref = x_all.at[pl.ds(1, SEPS - 1)]
        return remote(ref, ref, send.at[10], top_sem.at[5], next_z)

    def uc():
        return remote(tiles.at[other], tiles_core, send.at[11], top_sem.at[6], next_core)

    def ux(d):
        return remote(tiles.at[core, xy_of(TOP) + flip(d)], tiles_xy.at[d - 1],
                      send.at[12], top_sem.at[7], (leaf + 2 * flip(d), sep))

    def all_ux():
        return remote(tiles_xy, tiles_xy, send.at[12], top_sem.at[7], next_xy)

    def tg(d):
        return remote(tiles_res.at[0, 0], tiles_res.at[0, d],
                      send.at[13], top_sem.at[8], (leaf + 2 * flip(d), sep))

    def all_tg():
        ref = tiles_res.at[0, pl.ds(1, 15)]
        return remote(ref, ref, send.at[13], top_sem.at[8], next_xy)

    def tc():
        return remote(tiles_res.at[0], tiles_res.at[1], send.at[14], top_sem.at[9], next_core)

    def xo(d):
        return remote(x_out.at[z_peer(d)], x_in.at[d - 1], send.at[15], top_sem.at[10],
                      (leaf, z_peer(d)))

    def all_xo():
        return remote(x_in, x_in, send.at[15], top_sem.at[10], next_z)

    barrier = pltpu.get_barrier_semaphore()
    pl.semaphore_signal(barrier, inc=1, device_id=(partner, sep), device_id_type=MESH)
    for d in range(1, 16):
        pl.semaphore_signal(
            barrier, inc=1, device_id=(leaf + 2 * flip(d), sep), device_id_type=MESH)
    for d in range(1, SEPS):
        pl.semaphore_signal(
            barrier, inc=1, device_id=(leaf, z_peer(d)), device_id_type=MESH)

    inputs = [
        pltpu.make_async_copy(src, dst, sem_in.at[k])
        for k, (src, dst) in enumerate(
            [(inv_hbm, inv_ref), (rhs_hbm, rhs_ref), (srhs_hbm, srhs_ref)])]
    for copy in inputs:
        copy.start()
    load_w(0).start()
    load_d(0).start()
    load_c(0).start()
    load_w(1).start()
    load_d(1).start()
    load_c(1).start()
    load_w(2).start()
    load_d(2).start()
    load_c(2).start()
    load_w(3).start()

    for copy in inputs:
        copy.wait()
    live = lax.broadcasted_iota(jnp.int32, (RHS, CH), 1) < rows_ref[0, 0]
    right = jnp.where(live, rhs_ref[...].astype(F32), 0.0).astype(BF16)
    solved = jnp.dot(right, inv_ref[...], preferred_element_type=F32)
    solved = jnp.where(live, solved, 0.0)
    sol_ref[...] = solved.astype(BF16)
    leaf_copy = pltpu.make_async_copy(sol_ref, leaf_out, sem_in.at[3])
    leaf_copy.start()

    def turned_rows(scratch, value):
        scratch[...] = value.reshape(scratch.shape)
        return jnp.concatenate([scratch[z_peer(d)] for d in ORDER], axis=0)

    sol_rel[...] = turned_rows(turn_a, solved).astype(BF16)
    srhs_rel[...] = turned_rows(turn_b, srhs_ref[...].astype(F32)).astype(BF16)

    def terms_chunk(v, which_core, xy):
        m = 0 if v == 0 else 2 * xy + which_core
        block = 2 * (first_chunk(v) + m)
        col = column(v, which_core, xy)
        t = jnp.dot(sol_rel[...], weights[:, pl.ds(col, CH)], preferred_element_type=F32)
        left = t[:, :128] * (-mask_ref[block].astype(F32))
        rest = t[:, 128:] * (-mask_ref[block + 1].astype(F32))
        t = jnp.concatenate([left, rest], axis=1)
        part[place(v, which_core, xy)] = t.reshape(SEPS, 8, CH)

    def own_rows(v, rows_ref):
        r = lax.broadcasted_iota(jnp.int32, (LEVELS * 32, CH), 0)
        c = lax.broadcasted_iota(jnp.int32, (LEVELS * 32, CH), 1)
        pick = jnp.where((r - 32 * v == c - 32 * sep) & (r >= 32 * v) & (r < 32 * v + 32), 1.0, 0.0)
        own = jnp.dot(rows_ref[...], pick.astype(BF16), preferred_element_type=F32)
        return own.reshape(SEPS, 8, CH)

    def tile_place(j, g):
        return first_chunk(TOP) + (g % 2) * 2 ** (TOP - 1) + j * 4 + g // 2

    def top_terms():
        def some(at, carry):
            for j in range(TOP_CHUNKS):
                m = at * TOP_CHUNKS + j
                block = 2 * (first_chunk(TOP) + m)
                col = pl.multiple_of((first_chunk(TOP) + m) * CH, CH)
                t = jnp.dot(sol_ref[...], weights[:, pl.ds(col, CH)], preferred_element_type=F32)
                left = t[:, :128] * (-mask_ref[block].astype(F32))
                rest = t[:, 128:] * (-mask_ref[block + 1].astype(F32))
                t = jnp.concatenate([left, rest], axis=1)
                for g in range(8):
                    part[tile_place(j, g), at] = t[8 * g : 8 * g + 8]
            return carry

        lax.fori_loop(0, SEPS, some, 0)
        own = own_rows(TOP, srhs_ref)
        at = leaf // TOP_CHUNKS
        j = lax.rem(leaf, TOP_CHUNKS)
        for g in range(8):
            k = tile_place(j, g)
            part[k, at] = part[k, at] + own[g]

    def terms(v):
        if v == 0:
            terms_chunk(0, 0, 0)
        else:
            n = 2 ** (v - 1)
            step = min(n, 2)

            def some(i, carry):
                for j in range(step):
                    for c in range(2):
                        terms_chunk(v, c, i * step + j)
                return carry

            if n == step:
                some(0, 0)
            else:
                lax.fori_loop(0, n // step, some, 0)
        at = mine(v)
        part[at] = part[at] + own_rows(v, srhs_rel)

    def stack(src, dst, start, size):
        cols = pl.ds(pl.multiple_of(start, CH), size)
        hi, lo = split(src[:, cols])
        dst[0:32, cols] = hi
        dst[32:64, cols] = lo
        dst[64:96, cols] = hi
        dst[96:128, cols] = lo

    def stack_all(src, dst, start, size):
        width = min(size, 512)
        if size == width:
            stack(src, dst, start, size)
        else:
            def some(i, carry):
                stack(src, dst, start + i * width, width)
                return carry
            lax.fori_loop(0, size // width, some, 0)

    def prep(v):
        stack_all(dfull, dstack, first_chunk(v) * CH, 2**v * CH)
        if v:
            stack_all(cfull, cstack, (first_chunk(v) - 1) * CH, 2**v * CH)

    lanes = lax.broadcasted_iota(jnp.int32, (RHS, 128), 1)

    def product(v, which_core, xy, at, acc):
        hi, lo = split(resid[at].reshape(RHS, CH))
        rows = jnp.concatenate([hi, lo], axis=0)
        col = column(v, which_core, xy)
        return acc + lax.dot_general(
            rows, dstack[:, pl.ds(col, CH)], (((1,), (1,)), ((), ())),
            preferred_element_type=F32)

    def couple_chunk(v, xs, which_core, xy):
        at = place(v, which_core, xy)
        col = (first_chunk(v) - 1 + 2 * xy + which_core) * CH
        t = jnp.dot(xs, cstack[:, pl.ds(pl.multiple_of(col, CH), CH)], preferred_element_type=F32)
        part[at] = part[at] - t.reshape(SEPS, 8, CH)

    load_w(0).wait()
    terms(0)
    z_out[0] = part[0]
    pl.semaphore_wait(barrier, 1 + 15 + 7)

    quarter = lax.broadcasted_iota(jnp.int32, (16, 128), 1) // 32

    def top_xy(some):
        for d in some:
            i = xy_of(TOP) + flip(d)
            at = place(TOP, core, i)
            part[at] = part[at] + core_in[core_slot(TOP) + i]
            xr(TOP, d, None).start()

    def top_sum():
        i = xy_of(TOP)
        all_xr(TOP, None).wait_recv()
        total = part[mine(TOP)] + core_in[core_slot(TOP) + i]
        for d in range(1, 16):
            total = total + xy_in[xy_slot(TOP) + d - 1]
        z_out[TOP] = total

    def spread_sent(v):
        all_zg_sent(v).wait_send()
        if v >= 1:
            all_cg(v).wait_send()
        if v >= 2:
            all_xg_sent(v).wait_send()

    for v in range(TOP):
        if v >= 1:
            n = 2 ** (v - 1)
            step = min(n, 4)

            def theirs(i, carry):
                for j in range(step):
                    couple_chunk(v, xs, other, i * step + j)
                    cr(v, i * step + j).start()
                return carry

            def ours(i, carry):
                for j in range(step):
                    couple_chunk(v, xs, core, i * step + j)
                return carry

            if n == step:
                theirs(0, 0)
                ours(0, 0)
            else:
                lax.fori_loop(0, n // step, theirs, 0)
                lax.fori_loop(0, n // step, ours, 0)
            all_cr(v).wait_recv()
            for d in peers(v):
                i = xy_of(v) + flip(d)
                at = place(v, core, i)
                part[at] = part[at] + core_in[core_slot(v) + i]
                xr(v, d, 0).start()
            for g in range(1, 3):
                for d in peers(v):
                    xr(v, d, g).start()
            i = xy_of(v)
            at = mine(v)
            part[at] = part[at] + core_in[core_slot(v) + i]
            for g, (first, count) in enumerate(GROUPS):
                total = part[at, first : first + count]
                if v >= 2:
                    all_xr(v, g).wait_recv()
                for d in peers(v):
                    total = total + xy_in[xy_slot(v) + d - 1, first : first + count]
                z_out[v, first : first + count] = total
                for d in ORDER[first : first + count]:
                    if d:
                        zr(v, d).start()
        else:
            for d in ORDER[:-1]:
                zr(v, d).start()
        if v == 0:
            load_d(0).wait()
            load_c(0).wait()
            prep(0)
            load_w(1).wait()
            terms(1)
            prep(1)
            terms(2)
        elif v == 1:
            load_c(2).wait()
            load_d(2).wait()
            load_d(1).wait()
            load_c(1).wait()
            fire(v, "z")
            prep(2)
            load_w(3).wait()
            top_terms()
            for i in range(2 ** (TOP - 1)):
                cr(TOP, i).start()
        elif v == 2:
            prep(3)
            fire(v, "z")
            top_xy(range(8, 16))
        elif v == 3:
            fire(v, "z")
            prep(4)
            top_sum()
        else:
            fire(v, "z")
        if v >= 1:
            spread_sent(v - 1)
            all_cr(v).wait_send()
            if v >= 2:
                all_xr_sent(v).wait_send()
        total = z_out[v, SEPS - 1]
        all_zr(v).wait_recv()
        for d in range(1, SEPS):
            total = total + z_in[v, d - 1]
        resid[mine(v), SEPS - 1] = total
        for d in ORDER[:-1]:
            zg(v, d).start()
        fire(v, "g")
        if v == 0:
            load_w(2).wait()
            terms(3)
        elif v == 1:
            terms(4)
            all_cr(TOP).wait_recv()
            top_xy(range(1, 8))
        elif v == 4:
            all_zr(TOP).wait_recv()
        all_zr(v).wait_send()
        for g, (first, count) in reversed(list(enumerate(GROUPS))):
            all_zg(v, g).wait_recv()
            for d in peers(v):
                xg(v, d, g).start()
        if v >= 1:
            cg(v, 0).start()
        if v == 3:
            for d in range(1, SEPS):
                zr(TOP, d).start()
        fire(v, "x")
        if v == 4:
            wide_prep(C)
        acc = jnp.zeros((2 * RHS, 128), F32)
        if v == 0:
            acc = product(0, 0, 0, 0, acc)
        else:
            acc = product(v, core, xy_of(v), mine(v), acc)
            for d in peers(v):
                all_xg(v, d).wait_recv()
                cg(v, d).start()
                i = xy_of(v) + flip(d)
                acc = product(v, core, i, place(v, core, i), acc)
            all_cg(v).wait_recv()
            for d in range(2 ** (v - 1)):
                i = xy_of(v) + flip(d)
                acc = product(v, other, i, place(v, other, i), acc)
        t = acc[:RHS] + acc[RHS:]
        x = t + pltpu.roll(t, 32, 1)
        if v == TOP - 1:
            for p, d in enumerate(ORDER):
                turn_a[z_peer(d), :, :128] = x[8 * p : 8 * p + 8]
            x = turn_a[:, :, :128].reshape(RHS, 128)
            x_all[0] = functools.reduce(
                lambda kept, b: jnp.where(quarter == b, x[16 * b : 16 * b + 16], kept),
                range(1, 4), x[:16])
            for d in ORDER[:-1]:
                xa(d).start()
        if v < 4:
            old = jnp.zeros_like(x) if v == 0 else sep_rel[...]
            sep_rel[...] = jnp.where(lanes // 32 == v, x, old)
        else:
            sep_out[:, 32 * v : 32 * v + 32] = x[:, 32 * (v - 4) : 32 * (v - 3)]
        if v < TOP - 1:
            hi, lo = split(x)
            xs = jnp.where(lanes < 64, hi.astype(F32), lo.astype(F32)).astype(BF16)

    for p, d in enumerate(ORDER):
        rows = pl.ds(pl.multiple_of(8 * z_peer(d), 8), 8)
        sep_out[rows, :128] = sep_rel[8 * p : 8 * p + 8]

    all_xa().wait_recv()
    fire(TOP, "x")

    def merged(pieces):
        return functools.reduce(
            lambda kept, b: jnp.where(quarter == b, pieces[b], kept), range(1, 4), pieces[0])

    def turned(tile, quarters):
        shift = 32 * (quarters % 4)
        return pltpu.roll(tile, shift, 1) if shift else tile

    below = [x_all[lax.rem(sep + SEPS - s, SEPS)] for s in range(SEPS)]
    x = jnp.concatenate([
        jnp.concatenate([merged([turned(below[4 * h + q], q - b) for q in range(4)])
                         for b in range(4)], axis=0)
        for h in range(2)], axis=1)
    hi, lo = split(x)
    both = jnp.concatenate([hi, lo], axis=0)
    for j in range(TOP_CHUNKS):
        cols = slice(j * CH, j * CH + CH)
        t = jnp.dot(both, wide_hi[C, :, cols], preferred_element_type=F32)
        t = t[:RHS] + t[RHS:] + jnp.dot(hi, wide_lo[C, :, cols], preferred_element_type=F32)
        for g in range(8):
            tiles[g % 2, j * 4 + g // 2] = -t[8 * g : 8 * g + 8]
    uc().start()
    uc().wait_recv()
    for d in range(1, 16):
        at = xy_of(TOP) + flip(d)
        tiles[core, at] = tiles[core, at] + tiles_core[at]
        ux(d).start()
    at = xy_of(TOP)
    total = z_out[TOP, sep] + (tiles[core, at] + tiles_core[at])
    for d in range(1, SEPS):
        total = total + z_in[TOP, d - 1]
    all_ux().wait_recv()
    for d in range(1, 16):
        total = total + tiles_xy[d - 1]
    tiles_res[0, 0] = total
    for d in range(1, 16):
        tg(d).start()
    wide_prep(D)
    all_tg().wait_recv()
    tc().start()
    tc().wait_recv()

    def tile(j, g):
        xy = j * 4 + g // 2
        slot = sum(2**k * (1 - bits[k] if xy >> k & 1 else bits[k]) for k in range(4))
        return tiles_res[other if g % 2 else core, slot]

    solved_top = jnp.zeros((RHS, CH), F32)
    dims = (((1,), (1,)), ((), ()))
    for j in range(TOP_CHUNKS):
        cols = slice(j * CH, j * CH + CH)
        hi, lo = split(jnp.concatenate([tile(j, g) for g in range(8)], axis=0))
        both = jnp.concatenate([hi, lo], axis=0)
        t = lax.dot_general(both, wide_hi[D, :, cols], dims, preferred_element_type=F32)
        solved_top = solved_top + t[:RHS] + t[RHS:] + lax.dot_general(
            hi, wide_lo[D, :, cols], dims, preferred_element_type=F32)
    for h in range(2):
        rows = [solved_top[16 * b : 16 * b + 16, 128 * h : 128 * h + 128] for b in range(4)]
        for q in range(4):
            x_out[4 * h + q] = merged([turned(rows[b], b - q) for b in range(4)])
    for d in ORDER[:-1]:
        xo(d).start()
    spread_sent(TOP - 1)
    all_xa().wait_send()
    all_wide(C).wait_send()
    all_wide(D).wait_send()
    all_zr(TOP).wait_send()
    all_cr(TOP).wait_send()
    all_xr(TOP, None).wait_send()
    uc().wait_send()
    all_ux().wait_send()
    all_tg().wait_send()
    tc().wait_send()
    all_xo().wait_recv()
    total = x_out[sep]
    for d in range(1, SEPS):
        total = total + x_in[d - 1]
    for b in range(4):
        sep_out[16 * b : 16 * b + 16, 32 * TOP : 32 * TOP + 32] = turned(total, 1 - b)[:, 32:64]
    all_xo().wait_send()
    leaf_copy.wait()


def body(
    leaf_rhs, leaf_inv, leaf_coupling, block_mask, leaf_rows, sep_rhs, dinv_rows, sep_coupling
):
    sums = leaf_coupling.shape[3]
    parents = sep_coupling.shape[3]
    dma = pltpu.SemaphoreType.DMA
    vmem = pl.BlockSpec(memory_space=pltpu.VMEM)
    smem = pl.BlockSpec(memory_space=pltpu.SMEM)
    hbm = pl.BlockSpec(memory_space=pl.ANY)
    leaf_solution, sep_solution = pl.pallas_call(
        kernel,
        out_shape=(
            jax.ShapeDtypeStruct((RHS, CH), BF16),
            jax.ShapeDtypeStruct((RHS, LEVELS * 32), F32),
        ),
        in_specs=[smem, smem, hbm, hbm, hbm, hbm, hbm, hbm],
        out_specs=(hbm, vmem),
        scratch_shapes=[
            pltpu.VMEM((RHS, CH), BF16),
            pltpu.VMEM((CH, CH), BF16),
            pltpu.VMEM((RHS, LEVELS * 32), BF16),
            pltpu.VMEM((CH, sums), BF16),
            pltpu.VMEM((32, sums), F32),
            pltpu.VMEM((32, parents), F32),
            pltpu.VMEM((128, sums), BF16),
            pltpu.VMEM((128, parents), BF16),
            pltpu.VMEM((63, SEPS, 8, CH), F32),
            pltpu.VMEM((31, SEPS, 8, CH), F32),
            pltpu.VMEM((26, SEPS, 8, CH), F32),
            pltpu.VMEM((LEVELS, SEPS, 8, CH), F32),
            pltpu.VMEM((LEVELS, SEPS - 1, 8, CH), F32),
            pltpu.VMEM((63, SEPS, 8, CH), F32),
            pltpu.VMEM((RHS, CH), BF16),
            pltpu.VMEM((SEPS, 8, CH), F32),
            pltpu.VMEM((SEPS, 8, LEVELS * 32), F32),
            pltpu.VMEM((RHS, CH), BF16),
            pltpu.VMEM((RHS, LEVELS * 32), BF16),
            pltpu.VMEM((RHS, 128), F32),
            pltpu.VMEM((2, SEPS - 1, 32, TOP_CHUNKS * CH), F32),
            pltpu.VMEM((2, CH, TOP_CHUNKS * CH), BF16),
            pltpu.VMEM((2, CH, TOP_CHUNKS * CH), BF16),
            pltpu.VMEM((SEPS, 16, 128), F32),
            pltpu.VMEM((2, 16, 8, CH), F32),
            pltpu.VMEM((16, 8, CH), F32),
            pltpu.VMEM((15, 8, CH), F32),
            pltpu.VMEM((2, 16, 8, CH), F32),
            pltpu.VMEM((SEPS, 16, 128), F32),
            pltpu.VMEM((SEPS - 1, 16, 128), F32),
            dma((4,)), dma((4,)), dma((3,)), dma((3,)), dma((16,)), dma((4,)), dma((2,)), dma((3, 3)), dma((7,)),
            dma((11,)),
        ],
        compiler_params=pltpu.CompilerParams(
            collective_id=0, has_side_effects=True, vmem_limit_bytes=60 * 2**20),
        name="forward_substitution",
    )(
        block_mask[0, 0], leaf_rows, leaf_rhs[:, 0, 0, :], leaf_inv[0, 0], sep_rhs[:, 0, 0, :],
        leaf_coupling[0, 0], dinv_rows[0, 0], sep_coupling[0, 0],
    )
    return (leaf_solution[:, None, None, :], sep_solution[:, None, None, :])


def solution(mesh):
    return jax.shard_map(
        body,
        mesh=mesh,
        in_specs=(
            P(None, "leaf", "sep", None),
            P("leaf", "sep", None, None),
            P("leaf", "sep", None, None),
            P("leaf", "sep", None),
            P("leaf", "sep"),
            P(None, "leaf", "sep", None),
            P("leaf", "sep", None, None),
            P("leaf", "sep", None, None),
        ),
        out_specs=(P(None, "leaf", "sep", None), P(None, "leaf", "sep", None)),
        check_vma=False,
    )
```

```python
import functools

import jax
import jax.numpy as jnp
from jax import lax
from jax.experimental import pallas as pl
from jax.experimental.pallas import tpu as pltpu
from jax.sharding import PartitionSpec as P

MESH = pl.DeviceIdType.MESH
LEVELS = 6
SEPS = 8
TOP = LEVELS - 1
TOP_CHUNKS = 4
ORDER = (4, 3, 5, 2, 6, 1, 7, 0)
W_PARTS = (0, 1, 3, 5, 6)
D_PARTS = (0, 2, 5, 6)
C, D = 0, 1


def both_ways(a, d, *halves):
    return tuple((a, e, h) for h in halves or (0, 1) for e in sorted({d, SEPS - d}))


WIDE_COPIES = {
    (1, "z"): both_ways(C, 1),
    (1, "g"): both_ways(D, 1),
    (1, "x"): both_ways(C, 2),
    (2, "z"): both_ways(D, 2, 0),
    (2, "x"): both_ways(C, 3),
    (3, "z"): both_ways(D, 2, 1),
    (3, "x"): both_ways(C, 4),
    (4, "x"): both_ways(D, 4),
    (5, "x"): both_ways(D, 3),
}
GROUPS = ((0, 3), (3, 2), (5, 3))
RHS = 64
CH = 256
F32 = jnp.float32
BF16 = jnp.bfloat16


def first_chunk(v):
    return 2**v - 1


def xy_slot(v):
    return sum(2 ** (u - 1) - 1 for u in range(2, v))


def core_slot(v):
    return 2 ** (v - 1) - 1


def split(x):
    hi = x.astype(BF16)
    lo = (x - hi.astype(F32)).astype(BF16)
    return hi, lo


def kernel(
    mask_ref, rows_ref, rhs_hbm, inv_hbm, srhs_hbm, coup_hbm, dinv_hbm, scoup_hbm,
    leaf_out, sep_out,
    rhs_ref, inv_ref, srhs_ref,
    weights, dfull, cfull, dstack, cstack, part, core_in, xy_in, z_out, z_in, resid, sol_ref,
    turn_a, turn_b, sol_rel, srhs_rel, sep_rel,
    wide_in, wide_hi, wide_lo, x_all, tiles, tiles_core, tiles_xy, tiles_res, x_out, x_in,
    sem_in, sem_w, sem_d, sem_c, send, z_sem, core_sem, xr_sem, xg_sem, top_sem,
):
    leaf = lax.axis_index("leaf")
    sep = lax.axis_index("sep")
    core = lax.rem(leaf, 2)
    other = 1 - core
    bits = [lax.rem(leaf // 2 ** (k + 1), 2) for k in range(4)]
    partner = leaf + 1 - 2 * core

    def xy_of(v):
        return lax.rem(leaf // 2, 2 ** (v - 1))

    def flip(d):
        return sum(2**k * (1 - 2 * bits[k]) for k in range(4) if d >> k & 1)

    def place(v, which_core, xy):
        if v == 0:
            return 0
        return first_chunk(v) + which_core * 2 ** (v - 1) + xy

    def mine(v):
        return 0 if v == 0 else place(v, core, xy_of(v))

    def column(v, which_core, xy):
        if v == 0:
            return 0
        return pl.multiple_of((first_chunk(v) + 2 * xy + which_core) * CH, CH)

    def peers(v):
        return range(1, 2 ** (v - 1)) if v >= 2 else range(0)

    def load_w(k):
        cols = pl.ds(first_chunk(W_PARTS[k]) * CH,
                     (first_chunk(W_PARTS[k + 1]) - first_chunk(W_PARTS[k])) * CH)
        return pltpu.make_async_copy(coup_hbm.at[:, cols], weights.at[:, cols], sem_w.at[k])

    def load_d(k):
        cols = pl.ds(first_chunk(D_PARTS[k]) * CH,
                     (first_chunk(D_PARTS[k + 1]) - first_chunk(D_PARTS[k])) * CH)
        return pltpu.make_async_copy(dinv_hbm.at[:, cols], dfull.at[:, cols], sem_d.at[k])

    def load_c(k):
        start = max(first_chunk(D_PARTS[k]) - 1, 0)
        cols = pl.ds(start * CH, (first_chunk(D_PARTS[k + 1]) - 1 - start) * CH)
        return pltpu.make_async_copy(scoup_hbm.at[:, cols], cfull.at[:, cols], sem_c.at[k])

    def remote(src, dst, sent, arrived, to):
        return pltpu.make_async_remote_copy(
            src_ref=src, dst_ref=dst, send_sem=sent, recv_sem=arrived,
            device_id=to, device_id_type=MESH)

    def z_peer(d):
        return lax.rem(sep + d, SEPS)

    next_z = (leaf, z_peer(1))
    next_core = (partner, sep)
    next_xy = (leaf + 2 * flip(1), sep)

    def zr(v, d):
        top = v == TOP
        return remote(z_out.at[v, z_peer(d) if top else ORDER.index(d)], z_in.at[v, d - 1],
                      send.at[1 if top else 0], top_sem.at[0] if top else z_sem.at[0],
                      (leaf, z_peer(d)))

    def all_zr(v):
        top = v == TOP
        return remote(z_in.at[v], z_in.at[v], send.at[1 if top else 0],
                      top_sem.at[0] if top else z_sem.at[0], next_z)

    def zg(v, d):
        there = ORDER.index(SEPS - d)
        g = [first <= there < first + count for first, count in GROUPS].index(True)
        return remote(resid.at[mine(v), SEPS - 1], resid.at[mine(v), there],
                      send.at[2], z_sem.at[1 + g], (leaf, z_peer(d)))

    def all_zg(v, g):
        first, count = GROUPS[g]
        rows = resid.at[mine(v), pl.ds(first, count - (g == 2))]
        return remote(rows, rows, send.at[2], z_sem.at[1 + g], next_z)

    def all_zg_sent(v):
        return remote(z_in.at[v], z_in.at[v], send.at[2], z_sem.at[1], next_z)

    def rows_of(g):
        return pl.ds(*GROUPS[g])

    def xr(v, d, g):
        k = xy_slot(v) + d - 1
        at = place(v, core, xy_of(v) + flip(d))
        to = (leaf + 2 * flip(d), sep)
        if v == TOP:
            return remote(part.at[at], xy_in.at[k], send.at[4], top_sem.at[1], to)
        return remote(part.at[at, rows_of(g)], xy_in.at[k, rows_of(g)],
                      send.at[3], xr_sem.at[v - 2, g], to)

    def all_xr(v, g):
        slots = pl.ds(xy_slot(v), len(peers(v)))
        if v == TOP:
            ref = xy_in.at[slots]
            return remote(ref, ref, send.at[4], top_sem.at[1], next_xy)
        ref = xy_in.at[slots, rows_of(g)]
        return remote(ref, ref, send.at[3], xr_sem.at[v - 2, g], next_xy)

    def all_xr_sent(v):
        ref = xy_in.at[pl.ds(xy_slot(v), len(peers(v)))]
        return remote(ref, ref, send.at[3], xr_sem.at[v - 2, 0], next_xy)

    def xg(v, d, g):
        at = mine(v)
        return remote(resid.at[at, rows_of(g)], resid.at[at, rows_of(g)],
                      send.at[5], xg_sem.at[d - 1], (leaf + 2 * flip(d), sep))

    def all_xg(v, d):
        ref = resid.at[place(v, core, xy_of(v) + flip(d))]
        return remote(ref, ref, send.at[5], xg_sem.at[d - 1], (leaf + 2 * flip(d), sep))

    def all_xg_sent(v):
        ref = xy_in.at[pl.ds(xy_slot(v), len(peers(v)))]
        return remote(ref, ref, send.at[5], xg_sem.at[0], next_xy)

    def cr(v, i):
        top = v == TOP
        return remote(part.at[place(v, other, i)], core_in.at[core_slot(v) + i],
                      send.at[7 if top else 6], top_sem.at[2] if top else core_sem.at[0],
                      next_core)

    def all_cr(v):
        top = v == TOP
        ref = core_in.at[pl.ds(core_slot(v), 2 ** (v - 1))]
        return remote(ref, ref, send.at[7 if top else 6],
                      top_sem.at[2] if top else core_sem.at[0], next_core)

    def cg(v, d):
        ref = resid.at[place(v, core, xy_of(v) + flip(d))]
        return remote(ref, ref, send.at[8], core_sem.at[1], next_core)

    def all_cg(v):
        ref = resid.at[pl.ds(place(v, other, 0), 2 ** (v - 1))]
        return remote(ref, ref, send.at[8], core_sem.at[1], next_core)

    def wide(a, d, half):
        src, first = ((cfull, first_chunk(TOP) - 1), (dfull, first_chunk(TOP)))[a]
        to = z_peer(d)
        size = TOP_CHUNKS * CH // 2
        cols = pl.ds(pl.multiple_of((first + to * TOP_CHUNKS) * CH + half * size, CH), size)
        return remote(src.at[:, cols], wide_in.at[a, d - 1, :, pl.ds(half * size, size)],
                      send.at[9], top_sem.at[3 + a], (leaf, to))

    def all_wide(a):
        return remote(wide_in.at[a], wide_in.at[a], send.at[9], top_sem.at[3 + a], next_z)

    def fire(v, point):
        for piece in WIDE_COPIES.get((v, point), ()):
            wide(*piece).start()

    def wide_stack(a, at, block):
        rows = pl.ds(pl.multiple_of(at * 32, 32), 32)
        hi, lo = split(block)
        wide_hi[a, rows, :] = hi
        wide_lo[a, rows, :] = lo

    def wide_prep(a):
        src, first = ((cfull, first_chunk(TOP) - 1), (dfull, first_chunk(TOP)))[a]
        cols = pl.ds(pl.multiple_of((first + sep * TOP_CHUNKS) * CH, CH), TOP_CHUNKS * CH)
        wide_stack(a, sep, src[:, cols])
        all_wide(a).wait_recv()
        for d in range(1, SEPS):
            wide_stack(a, z_peer(SEPS - d), wide_in[a, d - 1])

    def xa(d):
        return remote(x_all.at[0], x_all.at[d], send.at[10], top_sem.at[5], (leaf, z_peer(d)))

    def all_xa():
        ref = x_all.at[pl.ds(1, SEPS - 1)]
        return remote(ref, ref, send.at[10], top_sem.at[5], next_z)

    def uc():
        return remote(tiles.at[other], tiles_core, send.at[11], top_sem.at[6], next_core)

    def ux(d):
        return remote(tiles.at[core, xy_of(TOP) + flip(d)], tiles_xy.at[d - 1],
                      send.at[12], top_sem.at[7], (leaf + 2 * flip(d), sep))

    def all_ux():
        return remote(tiles_xy, tiles_xy, send.at[12], top_sem.at[7], next_xy)

    def tg(d):
        return remote(tiles_res.at[0, 0], tiles_res.at[0, d],
                      send.at[13], top_sem.at[8], (leaf + 2 * flip(d), sep))

    def all_tg():
        ref = tiles_res.at[0, pl.ds(1, 15)]
        return remote(ref, ref, send.at[13], top_sem.at[8], next_xy)

    def tc():
        return remote(tiles_res.at[0], tiles_res.at[1], send.at[14], top_sem.at[9], next_core)

    def xo(d):
        return remote(x_out.at[z_peer(d)], x_in.at[d - 1], send.at[15], top_sem.at[10],
                      (leaf, z_peer(d)))

    def all_xo():
        return remote(x_in, x_in, send.at[15], top_sem.at[10], next_z)

    barrier = pltpu.get_barrier_semaphore()
    for d in ORDER[:-1]:
        pl.semaphore_signal(
            barrier, inc=1, device_id=(leaf, z_peer(d)), device_id_type=MESH)
    for d in reversed(range(1, 16)):
        pl.semaphore_signal(
            barrier, inc=1, device_id=(leaf + 2 * flip(d), sep), device_id_type=MESH)
    pl.semaphore_signal(barrier, inc=1, device_id=(partner, sep), device_id_type=MESH)
    inputs = [
        pltpu.make_async_copy(src, dst, sem_in.at[k])
        for k, (src, dst) in enumerate(
            [(inv_hbm, inv_ref), (rhs_hbm, rhs_ref), (srhs_hbm, srhs_ref)])]
    for copy in inputs:
        copy.start()
    load_w(0).start()
    load_d(0).start()
    load_c(0).start()
    load_w(1).start()
    load_d(1).start()
    load_c(1).start()
    load_w(2).start()
    load_d(2).start()
    load_c(2).start()
    load_w(3).start()

    for copy in inputs:
        copy.wait()
    live = lax.broadcasted_iota(jnp.int32, (RHS, CH), 1) < rows_ref[0, 0]
    right = jnp.where(live, rhs_ref[...].astype(F32), 0.0).astype(BF16)
    solved = jnp.dot(right, inv_ref[...], preferred_element_type=F32)
    solved = jnp.where(live, solved, 0.0)
    sol_ref[...] = solved.astype(BF16)
    leaf_copy = pltpu.make_async_copy(sol_ref, leaf_out, sem_in.at[3])
    leaf_copy.start()

    def turned_rows(scratch, value):
        scratch[...] = value.reshape(scratch.shape)
        return jnp.concatenate([scratch[z_peer(d)] for d in ORDER], axis=0)

    sol_rel[...] = turned_rows(turn_a, solved).astype(BF16)
    srhs_rel[...] = turned_rows(turn_b, srhs_ref[...].astype(F32)).astype(BF16)

    def terms_chunk(v, which_core, xy):
        m = 0 if v == 0 else 2 * xy + which_core
        block = 2 * (first_chunk(v) + m)
        col = column(v, which_core, xy)
        t = jnp.dot(sol_rel[...], weights[:, pl.ds(col, CH)], preferred_element_type=F32)
        left = t[:, :128] * (-mask_ref[block].astype(F32))
        rest = t[:, 128:] * (-mask_ref[block + 1].astype(F32))
        t = jnp.concatenate([left, rest], axis=1)
        part[place(v, which_core, xy)] = t.reshape(SEPS, 8, CH)

    def own_rows(v, rows_ref):
        r = lax.broadcasted_iota(jnp.int32, (LEVELS * 32, CH), 0)
        c = lax.broadcasted_iota(jnp.int32, (LEVELS * 32, CH), 1)
        pick = jnp.where((r - 32 * v == c - 32 * sep) & (r >= 32 * v) & (r < 32 * v + 32), 1.0, 0.0)
        own = jnp.dot(rows_ref[...], pick.astype(BF16), preferred_element_type=F32)
        return own.reshape(SEPS, 8, CH)

    def tile_place(j, g):
        return first_chunk(TOP) + (g % 2) * 2 ** (TOP - 1) + j * 4 + g // 2

    def top_terms():
        def some(at, carry):
            for j in range(TOP_CHUNKS):
                m = at * TOP_CHUNKS + j
                block = 2 * (first_chunk(TOP) + m)
                col = pl.multiple_of((first_chunk(TOP) + m) * CH, CH)
                t = jnp.dot(sol_ref[...], weights[:, pl.ds(col, CH)], preferred_element_type=F32)
                left = t[:, :128] * (-mask_ref[block].astype(F32))
                rest = t[:, 128:] * (-mask_ref[block + 1].astype(F32))
                t = jnp.concatenate([left, rest], axis=1)
                for g in range(8):
                    part[tile_place(j, g), at] = t[8 * g : 8 * g + 8]
            return carry

        lax.fori_loop(0, SEPS, some, 0)
        own = own_rows(TOP, srhs_ref)
        at = leaf // TOP_CHUNKS
        j = lax.rem(leaf, TOP_CHUNKS)
        for g in range(8):
            k = tile_place(j, g)
            part[k, at] = part[k, at] + own[g]

    def terms(v):
        if v == 0:
            terms_chunk(0, 0, 0)
        else:
            n = 2 ** (v - 1)
            step = min(n, 2)

            def some(i, carry):
                for j in range(step):
                    for c in range(2):
                        terms_chunk(v, c, i * step + j)
                return carry

            if n == step:
                some(0, 0)
            else:
                lax.fori_loop(0, n // step, some, 0)
        at = mine(v)
        part[at] = part[at] + own_rows(v, srhs_rel)

    def stack(src, dst, start, size):
        cols = pl.ds(pl.multiple_of(start, CH), size)
        hi, lo = split(src[:, cols])
        dst[0:32, cols] = hi
        dst[32:64, cols] = lo
        dst[64:96, cols] = hi
        dst[96:128, cols] = lo

    def stack_all(src, dst, start, size):
        width = min(size, 512)
        if size == width:
            stack(src, dst, start, size)
        else:
            def some(i, carry):
                stack(src, dst, start + i * width, width)
                return carry
            lax.fori_loop(0, size // width, some, 0)

    def prep(v):
        stack_all(dfull, dstack, first_chunk(v) * CH, 2**v * CH)
        if v:
            stack_all(cfull, cstack, (first_chunk(v) - 1) * CH, 2**v * CH)

    lanes = lax.broadcasted_iota(jnp.int32, (RHS, 128), 1)

    def product(v, which_core, xy, at, acc):
        hi, lo = split(resid[at].reshape(RHS, CH))
        rows = jnp.concatenate([hi, lo], axis=0)
        col = column(v, which_core, xy)
        return acc + lax.dot_general(
            rows, dstack[:, pl.ds(col, CH)], (((1,), (1,)), ((), ())),
            preferred_element_type=F32)

    def couple_chunk(v, xs, which_core, xy):
        at = place(v, which_core, xy)
        col = (first_chunk(v) - 1 + 2 * xy + which_core) * CH
        t = jnp.dot(xs, cstack[:, pl.ds(pl.multiple_of(col, CH), CH)], preferred_element_type=F32)
        part[at] = part[at] - t.reshape(SEPS, 8, CH)

    load_w(0).wait()
    terms(0)
    z_out[0] = part[0]
    pl.semaphore_wait(barrier, 1 + 15 + 7)

    quarter = lax.broadcasted_iota(jnp.int32, (16, 128), 1) // 32

    def top_xy(some):
        for d in some:
            i = xy_of(TOP) + flip(d)
            at = place(TOP, core, i)
            part[at] = part[at] + core_in[core_slot(TOP) + i]
            xr(TOP, d, None).start()

    def top_sum():
        i = xy_of(TOP)
        all_xr(TOP, None).wait_recv()
        total = part[mine(TOP)] + core_in[core_slot(TOP) + i]
        for d in range(1, 16):
            total = total + xy_in[xy_slot(TOP) + d - 1]
        z_out[TOP] = total

    def spread_sent(v):
        all_zg_sent(v).wait_send()
        if v >= 1:
            all_cg(v).wait_send()
        if v >= 2:
            all_xg_sent(v).wait_send()

    for v in range(TOP):
        if v >= 1:
            n = 2 ** (v - 1)
            step = min(n, 4)

            def theirs(i, carry):
                for j in range(step):
                    couple_chunk(v, xs, other, i * step + j)
                    cr(v, i * step + j).start()
                return carry

            def ours(i, carry):
                for j in range(step):
                    couple_chunk(v, xs, core, i * step + j)
                return carry

            if n == step:
                theirs(0, 0)
                ours(0, 0)
            else:
                lax.fori_loop(0, n // step, theirs, 0)
                lax.fori_loop(0, n // step, ours, 0)
            all_cr(v).wait_recv()
            for d in peers(v):
                i = xy_of(v) + flip(d)
                at = place(v, core, i)
                part[at] = part[at] + core_in[core_slot(v) + i]
                xr(v, d, 0).start()
            for g in range(1, 3):
                for d in peers(v):
                    xr(v, d, g).start()
            i = xy_of(v)
            at = mine(v)
            part[at] = part[at] + core_in[core_slot(v) + i]
            for g, (first, count) in enumerate(GROUPS):
                total = part[at, first : first + count]
                if v >= 2:
                    all_xr(v, g).wait_recv()
                for d in peers(v):
                    total = total + xy_in[xy_slot(v) + d - 1, first : first + count]
                z_out[v, first : first + count] = total
                for d in ORDER[first : first + count]:
                    if d:
                        zr(v, d).start()
        else:
            for d in ORDER[:-1]:
                zr(v, d).start()
        if v == 0:
            load_d(0).wait()
            load_c(0).wait()
            prep(0)
            load_w(1).wait()
            terms(1)
            prep(1)
            terms(2)
        elif v == 1:
            load_c(2).wait()
            load_d(2).wait()
            load_d(1).wait()
            load_c(1).wait()
            fire(v, "z")
            prep(2)
            load_w(3).wait()
            top_terms()
            for i in range(2 ** (TOP - 1)):
                cr(TOP, i).start()
        elif v == 2:
            prep(3)
            fire(v, "z")
            top_xy(range(8, 16))
        elif v == 3:
            fire(v, "z")
            prep(4)
            top_sum()
        else:
            fire(v, "z")
        if v >= 1:
            spread_sent(v - 1)
            all_cr(v).wait_send()
            if v >= 2:
                all_xr_sent(v).wait_send()
        total = z_out[v, SEPS - 1]
        all_zr(v).wait_recv()
        for d in range(1, SEPS):
            total = total + z_in[v, d - 1]
        resid[mine(v), SEPS - 1] = total
        for d in ORDER[:-1]:
            zg(v, d).start()
        fire(v, "g")
        if v == 0:
            load_w(2).wait()
            terms(3)
        elif v == 1:
            terms(4)
            all_cr(TOP).wait_recv()
            top_xy(range(1, 8))
        elif v == 4:
            all_zr(TOP).wait_recv()
        all_zr(v).wait_send()
        for g, (first, count) in reversed(list(enumerate(GROUPS))):
            all_zg(v, g).wait_recv()
            for d in peers(v):
                xg(v, d, g).start()
        if v >= 1:
            cg(v, 0).start()
        if v == 3:
            for d in range(1, SEPS):
                zr(TOP, d).start()
        fire(v, "x")
        if v == 4:
            wide_prep(C)
        acc = jnp.zeros((2 * RHS, 128), F32)
        if v == 0:
            acc = product(0, 0, 0, 0, acc)
        else:
            acc = product(v, core, xy_of(v), mine(v), acc)
            for d in peers(v):
                all_xg(v, d).wait_recv()
                cg(v, d).start()
                i = xy_of(v) + flip(d)
                acc = product(v, core, i, place(v, core, i), acc)
            all_cg(v).wait_recv()
            for d in range(2 ** (v - 1)):
                i = xy_of(v) + flip(d)
                acc = product(v, other, i, place(v, other, i), acc)
        t = acc[:RHS] + acc[RHS:]
        x = t + pltpu.roll(t, 32, 1)
        if v == TOP - 1:
            for p, d in enumerate(ORDER):
                turn_a[z_peer(d), :, :128] = x[8 * p : 8 * p + 8]
            x = turn_a[:, :, :128].reshape(RHS, 128)
            x_all[0] = functools.reduce(
                lambda kept, b: jnp.where(quarter == b, x[16 * b : 16 * b + 16], kept),
                range(1, 4), x[:16])
            for d in ORDER[:-1]:
                xa(d).start()
        if v < 4:
            old = jnp.zeros_like(x) if v == 0 else sep_rel[...]
            sep_rel[...] = jnp.where(lanes // 32 == v, x, old)
        else:
            sep_out[:, 32 * v : 32 * v + 32] = x[:, 32 * (v - 4) : 32 * (v - 3)]
        if v < TOP - 1:
            hi, lo = split(x)
            xs = jnp.where(lanes < 64, hi.astype(F32), lo.astype(F32)).astype(BF16)

    for p, d in enumerate(ORDER):
        rows = pl.ds(pl.multiple_of(8 * z_peer(d), 8), 8)
        sep_out[rows, :128] = sep_rel[8 * p : 8 * p + 8]

    all_xa().wait_recv()

    def merged(pieces):
        return functools.reduce(
            lambda kept, b: jnp.where(quarter == b, pieces[b], kept), range(1, 4), pieces[0])

    def turned(tile, quarters):
        shift = 32 * (quarters % 4)
        return pltpu.roll(tile, shift, 1) if shift else tile

    below = [x_all[lax.rem(sep + SEPS - s, SEPS)] for s in range(SEPS)]
    x = jnp.concatenate([
        jnp.concatenate([merged([turned(below[4 * h + q], q - b) for q in range(4)])
                         for b in range(4)], axis=0)
        for h in range(2)], axis=1)
    hi, lo = split(x)
    both = jnp.concatenate([hi, lo], axis=0)
    for j in range(TOP_CHUNKS):
        cols = slice(j * CH, j * CH + CH)
        t = jnp.dot(both, wide_hi[C, :, cols], preferred_element_type=F32)
        t = t[:RHS] + t[RHS:] + jnp.dot(hi, wide_lo[C, :, cols], preferred_element_type=F32)
        for g in range(8):
            tiles[g % 2, j * 4 + g // 2] = -t[8 * g : 8 * g + 8]
    uc().start()
    fire(TOP, "x")
    uc().wait_recv()
    for d in range(1, 16):
        at = xy_of(TOP) + flip(d)
        tiles[core, at] = tiles[core, at] + tiles_core[at]
        ux(d).start()
    at = xy_of(TOP)
    total = z_out[TOP, sep] + (tiles[core, at] + tiles_core[at])
    for d in range(1, SEPS):
        total = total + z_in[TOP, d - 1]
    all_ux().wait_recv()
    for d in range(1, 16):
        total = total + tiles_xy[d - 1]
    tiles_res[0, 0] = total
    for d in range(1, 16):
        tg(d).start()
    wide_prep(D)
    all_tg().wait_recv()
    tc().start()
    tc().wait_recv()

    def tile(j, g):
        xy = j * 4 + g // 2
        slot = sum(2**k * (1 - bits[k] if xy >> k & 1 else bits[k]) for k in range(4))
        return tiles_res[other if g % 2 else core, slot]

    solved_top = jnp.zeros((RHS, CH), F32)
    dims = (((1,), (1,)), ((), ()))
    for j in range(TOP_CHUNKS):
        cols = slice(j * CH, j * CH + CH)
        hi, lo = split(jnp.concatenate([tile(j, g) for g in range(8)], axis=0))
        both = jnp.concatenate([hi, lo], axis=0)
        t = lax.dot_general(both, wide_hi[D, :, cols], dims, preferred_element_type=F32)
        solved_top = solved_top + t[:RHS] + t[RHS:] + lax.dot_general(
            hi, wide_lo[D, :, cols], dims, preferred_element_type=F32)
    for h in range(2):
        rows = [solved_top[16 * b : 16 * b + 16, 128 * h : 128 * h + 128] for b in range(4)]
        for q in range(4):
            x_out[4 * h + q] = merged([turned(rows[b], b - q) for b in range(4)])
    for d in ORDER[:-1]:
        xo(d).start()
    spread_sent(TOP - 1)
    all_xa().wait_send()
    all_wide(C).wait_send()
    all_wide(D).wait_send()
    all_zr(TOP).wait_send()
    all_cr(TOP).wait_send()
    all_xr(TOP, None).wait_send()
    uc().wait_send()
    all_ux().wait_send()
    all_tg().wait_send()
    tc().wait_send()
    all_xo().wait_recv()
    total = x_out[sep]
    for d in range(1, SEPS):
        total = total + x_in[d - 1]
    for b in range(4):
        sep_out[16 * b : 16 * b + 16, 32 * TOP : 32 * TOP + 32] = turned(total, 1 - b)[:, 32:64]
    all_xo().wait_send()
    leaf_copy.wait()


def body(
    leaf_rhs, leaf_inv, leaf_coupling, block_mask, leaf_rows, sep_rhs, dinv_rows, sep_coupling
):
    sums = leaf_coupling.shape[3]
    parents = sep_coupling.shape[3]
    dma = pltpu.SemaphoreType.DMA
    vmem = pl.BlockSpec(memory_space=pltpu.VMEM)
    smem = pl.BlockSpec(memory_space=pltpu.SMEM)
    hbm = pl.BlockSpec(memory_space=pl.ANY)
    leaf_solution, sep_solution = pl.pallas_call(
        kernel,
        out_shape=(
            jax.ShapeDtypeStruct((RHS, CH), BF16),
            jax.ShapeDtypeStruct((RHS, LEVELS * 32), F32),
        ),
        in_specs=[smem, smem, hbm, hbm, hbm, hbm, hbm, hbm],
        out_specs=(hbm, vmem),
        scratch_shapes=[
            pltpu.VMEM((RHS, CH), BF16),
            pltpu.VMEM((CH, CH), BF16),
            pltpu.VMEM((RHS, LEVELS * 32), BF16),
            pltpu.VMEM((CH, sums), BF16),
            pltpu.VMEM((32, sums), F32),
            pltpu.VMEM((32, parents), F32),
            pltpu.VMEM((128, sums), BF16),
            pltpu.VMEM((128, parents), BF16),
            pltpu.VMEM((63, SEPS, 8, CH), F32),
            pltpu.VMEM((31, SEPS, 8, CH), F32),
            pltpu.VMEM((26, SEPS, 8, CH), F32),
            pltpu.VMEM((LEVELS, SEPS, 8, CH), F32),
            pltpu.VMEM((LEVELS, SEPS - 1, 8, CH), F32),
            pltpu.VMEM((63, SEPS, 8, CH), F32),
            pltpu.VMEM((RHS, CH), BF16),
            pltpu.VMEM((SEPS, 8, CH), F32),
            pltpu.VMEM((SEPS, 8, LEVELS * 32), F32),
            pltpu.VMEM((RHS, CH), BF16),
            pltpu.VMEM((RHS, LEVELS * 32), BF16),
            pltpu.VMEM((RHS, 128), F32),
            pltpu.VMEM((2, SEPS - 1, 32, TOP_CHUNKS * CH), F32),
            pltpu.VMEM((2, CH, TOP_CHUNKS * CH), BF16),
            pltpu.VMEM((2, CH, TOP_CHUNKS * CH), BF16),
            pltpu.VMEM((SEPS, 16, 128), F32),
            pltpu.VMEM((2, 16, 8, CH), F32),
            pltpu.VMEM((16, 8, CH), F32),
            pltpu.VMEM((15, 8, CH), F32),
            pltpu.VMEM((2, 16, 8, CH), F32),
            pltpu.VMEM((SEPS, 16, 128), F32),
            pltpu.VMEM((SEPS - 1, 16, 128), F32),
            dma((4,)), dma((4,)), dma((3,)), dma((3,)), dma((16,)), dma((4,)), dma((2,)), dma((3, 3)), dma((7,)),
            dma((11,)),
        ],
        compiler_params=pltpu.CompilerParams(
            collective_id=0, has_side_effects=True, vmem_limit_bytes=60 * 2**20),
        name="forward_substitution",
    )(
        block_mask[0, 0], leaf_rows, leaf_rhs[:, 0, 0, :], leaf_inv[0, 0], sep_rhs[:, 0, 0, :],
        leaf_coupling[0, 0], dinv_rows[0, 0], sep_coupling[0, 0],
    )
    return (leaf_solution[:, None, None, :], sep_solution[:, None, None, :])


def solution(mesh):
    return jax.shard_map(
        body,
        mesh=mesh,
        in_specs=(
            P(None, "leaf", "sep", None),
            P("leaf", "sep", None, None),
            P("leaf", "sep", None, None),
            P("leaf", "sep", None),
            P("leaf", "sep"),
            P(None, "leaf", "sep", None),
            P("leaf", "sep", None, None),
            P("leaf", "sep", None, None),
        ),
        out_specs=(P(None, "leaf", "sep", None), P(None, "leaf", "sep", None)),
        check_vma=False,
    )
```

```python
import functools

import jax
import jax.numpy as jnp
from jax import lax
from jax.experimental import pallas as pl
from jax.experimental.pallas import tpu as pltpu
from jax.sharding import PartitionSpec as P

MESH = pl.DeviceIdType.MESH
LEVELS = 6
SEPS = 8
TOP = LEVELS - 1
TOP_CHUNKS = 4
ORDER = (4, 3, 5, 2, 6, 1, 7, 0)
W_PARTS = (0, 1, 3, 5, 6)
D_PARTS = (0, 2, 5, 6)
C, D = 0, 1


def both_ways(a, d, *halves):
    return tuple((a, e, h) for h in halves or (None,) for e in sorted({d, SEPS - d}))


WIDE_COPIES = {
    (1, "z"): both_ways(C, 1),
    (1, "g"): both_ways(D, 1),
    (1, "x"): both_ways(C, 2),
    (2, "z"): both_ways(D, 2, 0),
    (2, "x"): both_ways(C, 3),
    (3, "z"): both_ways(D, 2, 1),
    (3, "x"): both_ways(C, 4),
    (4, "x"): both_ways(D, 4),
    (5, "x"): both_ways(D, 3),
}
GROUPS = ((0, 3), (3, 2), (5, 3))
RHS = 64
CH = 256
F32 = jnp.float32
BF16 = jnp.bfloat16


def first_chunk(v):
    return 2**v - 1


def xy_slot(v):
    return sum(2 ** (u - 1) - 1 for u in range(2, v))


def core_slot(v):
    return 2 ** (v - 1) - 1


def split(x):
    hi = x.astype(BF16)
    lo = (x - hi.astype(F32)).astype(BF16)
    return hi, lo


def kernel(
    mask_ref, rows_ref, rhs_hbm, inv_hbm, srhs_hbm, coup_hbm, dinv_hbm, scoup_hbm,
    leaf_out, sep_out,
    rhs_ref, inv_ref, srhs_ref,
    weights, dfull, cfull, dstack, cstack, part, core_in, xy_in, z_out, z_in, resid, sol_ref,
    turn_a, turn_b, sol_rel, srhs_rel, sep_rel,
    wide_in, wide_hi, wide_lo, x_all, tiles, tiles_core, tiles_xy, tiles_res, x_out, x_in,
    sem_in, sem_w, sem_d, sem_c, send, z_sem, core_sem, xr_sem, xg_sem, top_sem,
):
    leaf = lax.axis_index("leaf")
    sep = lax.axis_index("sep")
    core = lax.rem(leaf, 2)
    other = 1 - core
    bits = [lax.rem(leaf // 2 ** (k + 1), 2) for k in range(4)]
    partner = leaf + 1 - 2 * core

    def xy_of(v):
        return lax.rem(leaf // 2, 2 ** (v - 1))

    def flip(d):
        return sum(2**k * (1 - 2 * bits[k]) for k in range(4) if d >> k & 1)

    def place(v, which_core, xy):
        if v == 0:
            return 0
        return first_chunk(v) + which_core * 2 ** (v - 1) + xy

    def mine(v):
        return 0 if v == 0 else place(v, core, xy_of(v))

    def column(v, which_core, xy):
        if v == 0:
            return 0
        return pl.multiple_of((first_chunk(v) + 2 * xy + which_core) * CH, CH)

    def peers(v):
        return range(1, 2 ** (v - 1)) if v >= 2 else range(0)

    def load_w(k):
        cols = pl.ds(first_chunk(W_PARTS[k]) * CH,
                     (first_chunk(W_PARTS[k + 1]) - first_chunk(W_PARTS[k])) * CH)
        return pltpu.make_async_copy(coup_hbm.at[:, cols], weights.at[:, cols], sem_w.at[k])

    def load_d(k):
        cols = pl.ds(first_chunk(D_PARTS[k]) * CH,
                     (first_chunk(D_PARTS[k + 1]) - first_chunk(D_PARTS[k])) * CH)
        return pltpu.make_async_copy(dinv_hbm.at[:, cols], dfull.at[:, cols], sem_d.at[k])

    def load_c(k):
        start = max(first_chunk(D_PARTS[k]) - 1, 0)
        cols = pl.ds(start * CH, (first_chunk(D_PARTS[k + 1]) - 1 - start) * CH)
        return pltpu.make_async_copy(scoup_hbm.at[:, cols], cfull.at[:, cols], sem_c.at[k])

    def remote(src, dst, sent, arrived, to):
        return pltpu.make_async_remote_copy(
            src_ref=src, dst_ref=dst, send_sem=sent, recv_sem=arrived,
            device_id=to, device_id_type=MESH)

    def z_peer(d):
        return lax.rem(sep + d, SEPS)

    next_z = (leaf, z_peer(1))
    next_core = (partner, sep)
    next_xy = (leaf + 2 * flip(1), sep)

    def zr(v, d):
        top = v == TOP
        return remote(z_out.at[v, z_peer(d) if top else ORDER.index(d)], z_in.at[v, d - 1],
                      send.at[1 if top else 0], top_sem.at[0] if top else z_sem.at[0],
                      (leaf, z_peer(d)))

    def all_zr(v):
        top = v == TOP
        return remote(z_in.at[v], z_in.at[v], send.at[1 if top else 0],
                      top_sem.at[0] if top else z_sem.at[0], next_z)

    def zg(v, d):
        there = ORDER.index(SEPS - d)
        g = [first <= there < first + count for first, count in GROUPS].index(True)
        return remote(resid.at[mine(v), SEPS - 1], resid.at[mine(v), there],
                      send.at[2], z_sem.at[1 + g], (leaf, z_peer(d)))

    def all_zg(v, g):
        first, count = GROUPS[g]
        rows = resid.at[mine(v), pl.ds(first, count - (g == 2))]
        return remote(rows, rows, send.at[2], z_sem.at[1 + g], next_z)

    def all_zg_sent(v):
        return remote(z_in.at[v], z_in.at[v], send.at[2], z_sem.at[1], next_z)

    def rows_of(g):
        return pl.ds(*GROUPS[g])

    def xr(v, d, g):
        k = xy_slot(v) + d - 1
        at = place(v, core, xy_of(v) + flip(d))
        to = (leaf + 2 * flip(d), sep)
        if v == TOP:
            return remote(part.at[at], xy_in.at[k], send.at[4], top_sem.at[1], to)
        return remote(part.at[at, rows_of(g)], xy_in.at[k, rows_of(g)],
                      send.at[3], xr_sem.at[v - 2, g], to)

    def all_xr(v, g):
        slots = pl.ds(xy_slot(v), len(peers(v)))
        if v == TOP:
            ref = xy_in.at[slots]
            return remote(ref, ref, send.at[4], top_sem.at[1], next_xy)
        ref = xy_in.at[slots, rows_of(g)]
        return remote(ref, ref, send.at[3], xr_sem.at[v - 2, g], next_xy)

    def all_xr_sent(v):
        ref = xy_in.at[pl.ds(xy_slot(v), len(peers(v)))]
        return remote(ref, ref, send.at[3], xr_sem.at[v - 2, 0], next_xy)

    def xg(v, d, g):
        at = mine(v)
        return remote(resid.at[at, rows_of(g)], resid.at[at, rows_of(g)],
                      send.at[5], xg_sem.at[d - 1], (leaf + 2 * flip(d), sep))

    def all_xg(v, d):
        ref = resid.at[place(v, core, xy_of(v) + flip(d))]
        return remote(ref, ref, send.at[5], xg_sem.at[d - 1], (leaf + 2 * flip(d), sep))

    def all_xg_sent(v):
        ref = xy_in.at[pl.ds(xy_slot(v), len(peers(v)))]
        return remote(ref, ref, send.at[5], xg_sem.at[0], next_xy)

    def cr(v, i):
        top = v == TOP
        return remote(part.at[place(v, other, i)], core_in.at[core_slot(v) + i],
                      send.at[7 if top else 6], top_sem.at[2] if top else core_sem.at[0],
                      next_core)

    def all_cr(v):
        top = v == TOP
        ref = core_in.at[pl.ds(core_slot(v), 2 ** (v - 1))]
        return remote(ref, ref, send.at[7 if top else 6],
                      top_sem.at[2] if top else core_sem.at[0], next_core)

    def cg(v, d):
        ref = resid.at[place(v, core, xy_of(v) + flip(d))]
        return remote(ref, ref, send.at[8], core_sem.at[1], next_core)

    def all_cg(v):
        ref = resid.at[pl.ds(place(v, other, 0), 2 ** (v - 1))]
        return remote(ref, ref, send.at[8], core_sem.at[1], next_core)

    def wide(a, d, half):
        src, first = ((cfull, first_chunk(TOP) - 1), (dfull, first_chunk(TOP)))[a]
        to = z_peer(d)
        size = TOP_CHUNKS * CH // (1 if half is None else 2)
        half = half or 0
        cols = pl.ds(pl.multiple_of((first + to * TOP_CHUNKS) * CH + half * size, CH), size)
        return remote(src.at[:, cols], wide_in.at[a, d - 1, :, pl.ds(half * size, size)],
                      send.at[9], top_sem.at[3 + a], (leaf, to))

    def all_wide(a):
        return remote(wide_in.at[a], wide_in.at[a], send.at[9], top_sem.at[3 + a], next_z)

    def fire(v, point):
        for piece in WIDE_COPIES.get((v, point), ()):
            wide(*piece).start()

    def wide_stack(a, at, block):
        rows = pl.ds(pl.multiple_of(at * 32, 32), 32)
        hi, lo = split(block)
        wide_hi[a, rows, :] = hi
        wide_lo[a, rows, :] = lo

    def wide_prep(a):
        src, first = ((cfull, first_chunk(TOP) - 1), (dfull, first_chunk(TOP)))[a]
        cols = pl.ds(pl.multiple_of((first + sep * TOP_CHUNKS) * CH, CH), TOP_CHUNKS * CH)
        wide_stack(a, sep, src[:, cols])
        all_wide(a).wait_recv()
        for d in range(1, SEPS):
            wide_stack(a, z_peer(SEPS - d), wide_in[a, d - 1])

    def xa(d):
        return remote(x_all.at[0], x_all.at[d], send.at[10], top_sem.at[5], (leaf, z_peer(d)))

    def all_xa():
        ref = x_all.at[pl.ds(1, SEPS - 1)]
        return remote(ref, ref, send.at[10], top_sem.at[5], next_z)

    def uc():
        return remote(tiles.at[other], tiles_core, send.at[11], top_sem.at[6], next_core)

    def uc_part(j):
        some = pl.ds(4 * j, 4)
        return remote(tiles.at[other, some], tiles_core.at[some],
                      send.at[11], top_sem.at[6], next_core)

    def ux(d):
        return remote(tiles.at[core, xy_of(TOP) + flip(d)], tiles_xy.at[d - 1],
                      send.at[12], top_sem.at[7], (leaf + 2 * flip(d), sep))

    def all_ux():
        return remote(tiles_xy, tiles_xy, send.at[12], top_sem.at[7], next_xy)

    def tg(d):
        return remote(tiles_res.at[0, 0], tiles_res.at[0, d],
                      send.at[13], top_sem.at[8], (leaf + 2 * flip(d), sep))

    def all_tg():
        ref = tiles_res.at[0, pl.ds(1, 15)]
        return remote(ref, ref, send.at[13], top_sem.at[8], next_xy)

    def tc():
        return remote(tiles_res.at[0], tiles_res.at[1], send.at[14], top_sem.at[9], next_core)

    def xo(d):
        return remote(x_out.at[z_peer(d)], x_in.at[d - 1], send.at[15], top_sem.at[10],
                      (leaf, z_peer(d)))

    def all_xo():
        return remote(x_in, x_in, send.at[15], top_sem.at[10], next_z)

    barrier = pltpu.get_barrier_semaphore()
    for d in ORDER[:-1]:
        pl.semaphore_signal(
            barrier, inc=1, device_id=(leaf, z_peer(d)), device_id_type=MESH)
    for d in reversed(range(1, 16)):
        pl.semaphore_signal(
            barrier, inc=1, device_id=(leaf + 2 * flip(d), sep), device_id_type=MESH)
    pl.semaphore_signal(barrier, inc=1, device_id=(partner, sep), device_id_type=MESH)
    inputs = [
        pltpu.make_async_copy(src, dst, sem_in.at[k])
        for k, (src, dst) in enumerate(
            [(inv_hbm, inv_ref), (rhs_hbm, rhs_ref), (srhs_hbm, srhs_ref)])]
    for copy in inputs:
        copy.start()
    load_w(0).start()
    load_d(0).start()
    load_c(0).start()
    load_w(1).start()
    load_d(1).start()
    load_c(1).start()
    load_w(2).start()
    load_d(2).start()
    load_c(2).start()
    load_w(3).start()

    for copy in inputs:
        copy.wait()
    live = lax.broadcasted_iota(jnp.int32, (RHS, CH), 1) < rows_ref[0, 0]
    right = jnp.where(live, rhs_ref[...].astype(F32), 0.0).astype(BF16)
    solved = jnp.dot(right, inv_ref[...], preferred_element_type=F32)
    solved = jnp.where(live, solved, 0.0)
    sol_ref[...] = solved.astype(BF16)
    leaf_copy = pltpu.make_async_copy(sol_ref, leaf_out, sem_in.at[3])
    leaf_copy.start()

    def turned_rows(scratch, value):
        scratch[...] = value.reshape(scratch.shape)
        return jnp.concatenate([scratch[z_peer(d)] for d in ORDER], axis=0)

    sol_rel[...] = turned_rows(turn_a, solved).astype(BF16)
    srhs_rel[...] = turned_rows(turn_b, srhs_ref[...].astype(F32)).astype(BF16)

    def terms_chunk(v, which_core, xy):
        m = 0 if v == 0 else 2 * xy + which_core
        block = 2 * (first_chunk(v) + m)
        col = column(v, which_core, xy)
        t = jnp.dot(sol_rel[...], weights[:, pl.ds(col, CH)], preferred_element_type=F32)
        left = t[:, :128] * (-mask_ref[block].astype(F32))
        rest = t[:, 128:] * (-mask_ref[block + 1].astype(F32))
        t = jnp.concatenate([left, rest], axis=1)
        part[place(v, which_core, xy)] = t.reshape(SEPS, 8, CH)

    def own_rows(v, rows_ref):
        r = lax.broadcasted_iota(jnp.int32, (LEVELS * 32, CH), 0)
        c = lax.broadcasted_iota(jnp.int32, (LEVELS * 32, CH), 1)
        pick = jnp.where((r - 32 * v == c - 32 * sep) & (r >= 32 * v) & (r < 32 * v + 32), 1.0, 0.0)
        own = jnp.dot(rows_ref[...], pick.astype(BF16), preferred_element_type=F32)
        return own.reshape(SEPS, 8, CH)

    def tile_place(j, g):
        return first_chunk(TOP) + (g % 2) * 2 ** (TOP - 1) + j * 4 + g // 2

    def top_terms():
        def some(at, carry):
            for j in range(TOP_CHUNKS):
                m = at * TOP_CHUNKS + j
                block = 2 * (first_chunk(TOP) + m)
                col = pl.multiple_of((first_chunk(TOP) + m) * CH, CH)
                t = jnp.dot(sol_ref[...], weights[:, pl.ds(col, CH)], preferred_element_type=F32)
                left = t[:, :128] * (-mask_ref[block].astype(F32))
                rest = t[:, 128:] * (-mask_ref[block + 1].astype(F32))
                t = jnp.concatenate([left, rest], axis=1)
                for g in range(8):
                    part[tile_place(j, g), at] = t[8 * g : 8 * g + 8]
            return carry

        lax.fori_loop(0, SEPS, some, 0)
        own = own_rows(TOP, srhs_ref)
        at = leaf // TOP_CHUNKS
        j = lax.rem(leaf, TOP_CHUNKS)
        for g in range(8):
            k = tile_place(j, g)
            part[k, at] = part[k, at] + own[g]

    def terms(v):
        if v == 0:
            terms_chunk(0, 0, 0)
        else:
            n = 2 ** (v - 1)
            step = min(n, 2)

            def some(i, carry):
                for j in range(step):
                    for c in range(2):
                        terms_chunk(v, c, i * step + j)
                return carry

            if n == step:
                some(0, 0)
            else:
                lax.fori_loop(0, n // step, some, 0)
        at = mine(v)
        part[at] = part[at] + own_rows(v, srhs_rel)

    def stack(src, dst, start, size):
        cols = pl.ds(pl.multiple_of(start, CH), size)
        hi, lo = split(src[:, cols])
        dst[0:32, cols] = hi
        dst[32:64, cols] = lo
        dst[64:96, cols] = hi
        dst[96:128, cols] = lo

    def stack_all(src, dst, start, size):
        width = min(size, 512)
        if size == width:
            stack(src, dst, start, size)
        else:
            def some(i, carry):
                stack(src, dst, start + i * width, width)
                return carry
            lax.fori_loop(0, size // width, some, 0)

    def prep(v):
        stack_all(dfull, dstack, first_chunk(v) * CH, 2**v * CH)
        if v:
            stack_all(cfull, cstack, (first_chunk(v) - 1) * CH, 2**v * CH)

    lanes = lax.broadcasted_iota(jnp.int32, (RHS, 128), 1)

    def product(v, which_core, xy, at, acc):
        hi, lo = split(resid[at].reshape(RHS, CH))
        rows = jnp.concatenate([hi, lo], axis=0)
        col = column(v, which_core, xy)
        return acc + lax.dot_general(
            rows, dstack[:, pl.ds(col, CH)], (((1,), (1,)), ((), ())),
            preferred_element_type=F32)

    def couple_chunk(v, xs, which_core, xy):
        at = place(v, which_core, xy)
        col = (first_chunk(v) - 1 + 2 * xy + which_core) * CH
        t = jnp.dot(xs, cstack[:, pl.ds(pl.multiple_of(col, CH), CH)], preferred_element_type=F32)
        part[at] = part[at] - t.reshape(SEPS, 8, CH)

    load_w(0).wait()
    terms(0)
    z_out[0] = part[0]
    pl.semaphore_wait(barrier, 1 + 15 + 7)

    quarter = lax.broadcasted_iota(jnp.int32, (16, 128), 1) // 32

    def top_xy(some):
        for d in some:
            i = xy_of(TOP) + flip(d)
            at = place(TOP, core, i)
            part[at] = part[at] + core_in[core_slot(TOP) + i]
            xr(TOP, d, None).start()

    def top_sum():
        i = xy_of(TOP)
        all_xr(TOP, None).wait_recv()
        total = part[mine(TOP)] + core_in[core_slot(TOP) + i]
        for d in range(1, 16):
            total = total + xy_in[xy_slot(TOP) + d - 1]
        z_out[TOP] = total

    def spread_sent(v):
        all_zg_sent(v).wait_send()
        if v >= 1:
            all_cg(v).wait_send()
        if v >= 2:
            all_xg_sent(v).wait_send()

    for v in range(TOP):
        if v >= 1:
            n = 2 ** (v - 1)
            step = min(n, 4)

            def theirs(i, carry):
                for j in range(step):
                    couple_chunk(v, xs, other, i * step + j)
                    cr(v, i * step + j).start()
                return carry

            def ours(i, carry):
                for j in range(step):
                    couple_chunk(v, xs, core, i * step + j)
                return carry

            if n == step:
                theirs(0, 0)
                ours(0, 0)
            else:
                lax.fori_loop(0, n // step, theirs, 0)
                lax.fori_loop(0, n // step, ours, 0)
            all_cr(v).wait_recv()
            for d in peers(v):
                i = xy_of(v) + flip(d)
                at = place(v, core, i)
                part[at] = part[at] + core_in[core_slot(v) + i]
                xr(v, d, 0).start()
            for g in range(1, 3):
                for d in peers(v):
                    xr(v, d, g).start()
            i = xy_of(v)
            at = mine(v)
            part[at] = part[at] + core_in[core_slot(v) + i]
            for g, (first, count) in enumerate(GROUPS):
                total = part[at, first : first + count]
                if v >= 2:
                    all_xr(v, g).wait_recv()
                for d in peers(v):
                    total = total + xy_in[xy_slot(v) + d - 1, first : first + count]
                z_out[v, first : first + count] = total
                for d in ORDER[first : first + count]:
                    if d:
                        zr(v, d).start()
        else:
            for d in ORDER[:-1]:
                zr(v, d).start()
        if v == 0:
            load_d(0).wait()
            load_c(0).wait()
            prep(0)
            load_w(1).wait()
            terms(1)
            prep(1)
            terms(2)
        elif v == 1:
            load_c(2).wait()
            load_d(2).wait()
            load_d(1).wait()
            load_c(1).wait()
            fire(v, "z")
            prep(2)
            load_w(3).wait()
            top_terms()
            for i in range(2 ** (TOP - 1)):
                cr(TOP, i).start()
        elif v == 2:
            prep(3)
            fire(v, "z")
            top_xy(range(8, 16))
        elif v == 3:
            fire(v, "z")
            prep(4)
            top_sum()
        else:
            fire(v, "z")
        if v >= 1:
            spread_sent(v - 1)
            all_cr(v).wait_send()
            if v >= 2:
                all_xr_sent(v).wait_send()
        total = z_out[v, SEPS - 1]
        all_zr(v).wait_recv()
        for d in range(1, SEPS):
            total = total + z_in[v, d - 1]
        resid[mine(v), SEPS - 1] = total
        for d in ORDER[:-1]:
            zg(v, d).start()
        fire(v, "g")
        if v == 0:
            load_w(2).wait()
            terms(3)
        elif v == 1:
            terms(4)
            all_cr(TOP).wait_recv()
            top_xy(range(1, 8))
        elif v == 4:
            all_zr(TOP).wait_recv()
        all_zr(v).wait_send()
        for g, (first, count) in reversed(list(enumerate(GROUPS))):
            all_zg(v, g).wait_recv()
            for d in peers(v):
                xg(v, d, g).start()
        if v >= 1:
            cg(v, 0).start()
        if v == 3:
            for d in range(1, SEPS):
                zr(TOP, d).start()
        fire(v, "x")
        if v == 4:
            wide_prep(C)
        acc = jnp.zeros((2 * RHS, 128), F32)
        if v == 0:
            acc = product(0, 0, 0, 0, acc)
        else:
            acc = product(v, core, xy_of(v), mine(v), acc)
            for d in peers(v):
                all_xg(v, d).wait_recv()
                cg(v, d).start()
                i = xy_of(v) + flip(d)
                acc = product(v, core, i, place(v, core, i), acc)
            all_cg(v).wait_recv()
            for d in range(2 ** (v - 1)):
                i = xy_of(v) + flip(d)
                acc = product(v, other, i, place(v, other, i), acc)
        t = acc[:RHS] + acc[RHS:]
        x = t + pltpu.roll(t, 32, 1)
        if v == TOP - 1:
            for p, d in enumerate(ORDER):
                turn_a[z_peer(d), :, :128] = x[8 * p : 8 * p + 8]
            x = turn_a[:, :, :128].reshape(RHS, 128)
            x_all[0] = functools.reduce(
                lambda kept, b: jnp.where(quarter == b, x[16 * b : 16 * b + 16], kept),
                range(1, 4), x[:16])
            for d in ORDER[:-1]:
                xa(d).start()
        if v < 4:
            old = jnp.zeros_like(x) if v == 0 else sep_rel[...]
            sep_rel[...] = jnp.where(lanes // 32 == v, x, old)
        else:
            sep_out[:, 32 * v : 32 * v + 32] = x[:, 32 * (v - 4) : 32 * (v - 3)]
        if v < TOP - 1:
            hi, lo = split(x)
            xs = jnp.where(lanes < 64, hi.astype(F32), lo.astype(F32)).astype(BF16)

    for p, d in enumerate(ORDER):
        rows = pl.ds(pl.multiple_of(8 * z_peer(d), 8), 8)
        sep_out[rows, :128] = sep_rel[8 * p : 8 * p + 8]

    all_xa().wait_recv()

    def merged(pieces):
        return functools.reduce(
            lambda kept, b: jnp.where(quarter == b, pieces[b], kept), range(1, 4), pieces[0])

    def turned(tile, quarters):
        shift = 32 * (quarters % 4)
        return pltpu.roll(tile, shift, 1) if shift else tile

    below = [x_all[lax.rem(sep + SEPS - s, SEPS)] for s in range(SEPS)]
    x = jnp.concatenate([
        jnp.concatenate([merged([turned(below[4 * h + q], q - b) for q in range(4)])
                         for b in range(4)], axis=0)
        for h in range(2)], axis=1)
    hi, lo = split(x)
    both = jnp.concatenate([hi, lo], axis=0)
    for j in range(TOP_CHUNKS):
        cols = slice(j * CH, j * CH + CH)
        t = jnp.dot(both, wide_hi[C, :, cols], preferred_element_type=F32)
        t = t[:RHS] + t[RHS:] + jnp.dot(hi, wide_lo[C, :, cols], preferred_element_type=F32)
        for g in range(8):
            tiles[g % 2, j * 4 + g // 2] = -t[8 * g : 8 * g + 8]
        uc_part(j).start()
    fire(TOP, "x")
    uc().wait_recv()
    for d in range(1, 16):
        at = xy_of(TOP) + flip(d)
        tiles[core, at] = tiles[core, at] + tiles_core[at]
        ux(d).start()
    at = xy_of(TOP)
    total = z_out[TOP, sep] + (tiles[core, at] + tiles_core[at])
    for d in range(1, SEPS):
        total = total + z_in[TOP, d - 1]
    all_ux().wait_recv()
    for d in range(1, 16):
        total = total + tiles_xy[d - 1]
    tiles_res[0, 0] = total
    for d in range(1, 16):
        tg(d).start()
    wide_prep(D)
    all_tg().wait_recv()
    tc().start()
    tc().wait_recv()

    def tile(j, g):
        xy = j * 4 + g // 2
        slot = sum(2**k * (1 - bits[k] if xy >> k & 1 else bits[k]) for k in range(4))
        return tiles_res[other if g % 2 else core, slot]

    solved_top = jnp.zeros((RHS, CH), F32)
    dims = (((1,), (1,)), ((), ()))
    for j in range(TOP_CHUNKS):
        cols = slice(j * CH, j * CH + CH)
        hi, lo = split(jnp.concatenate([tile(j, g) for g in range(8)], axis=0))
        both = jnp.concatenate([hi, lo], axis=0)
        t = lax.dot_general(both, wide_hi[D, :, cols], dims, preferred_element_type=F32)
        solved_top = solved_top + t[:RHS] + t[RHS:] + lax.dot_general(
            hi, wide_lo[D, :, cols], dims, preferred_element_type=F32)
    for h in range(2):
        rows = [solved_top[16 * b : 16 * b + 16, 128 * h : 128 * h + 128] for b in range(4)]
        for q in range(4):
            x_out[4 * h + q] = merged([turned(rows[b], b - q) for b in range(4)])
    for d in ORDER[:-1]:
        xo(d).start()
    spread_sent(TOP - 1)
    all_xa().wait_send()
    all_wide(C).wait_send()
    all_wide(D).wait_send()
    all_zr(TOP).wait_send()
    all_cr(TOP).wait_send()
    all_xr(TOP, None).wait_send()
    uc().wait_send()
    all_ux().wait_send()
    all_tg().wait_send()
    tc().wait_send()
    all_xo().wait_recv()
    total = x_out[sep]
    for d in range(1, SEPS):
        total = total + x_in[d - 1]
    for b in range(4):
        sep_out[16 * b : 16 * b + 16, 32 * TOP : 32 * TOP + 32] = turned(total, 1 - b)[:, 32:64]
    all_xo().wait_send()
    leaf_copy.wait()


def body(
    leaf_rhs, leaf_inv, leaf_coupling, block_mask, leaf_rows, sep_rhs, dinv_rows, sep_coupling
):
    sums = leaf_coupling.shape[3]
    parents = sep_coupling.shape[3]
    dma = pltpu.SemaphoreType.DMA
    vmem = pl.BlockSpec(memory_space=pltpu.VMEM)
    smem = pl.BlockSpec(memory_space=pltpu.SMEM)
    hbm = pl.BlockSpec(memory_space=pl.ANY)
    leaf_solution, sep_solution = pl.pallas_call(
        kernel,
        out_shape=(
            jax.ShapeDtypeStruct((RHS, CH), BF16),
            jax.ShapeDtypeStruct((RHS, LEVELS * 32), F32),
        ),
        in_specs=[smem, smem, hbm, hbm, hbm, hbm, hbm, hbm],
        out_specs=(hbm, vmem),
        scratch_shapes=[
            pltpu.VMEM((RHS, CH), BF16),
            pltpu.VMEM((CH, CH), BF16),
            pltpu.VMEM((RHS, LEVELS * 32), BF16),
            pltpu.VMEM((CH, sums), BF16),
            pltpu.VMEM((32, sums), F32),
            pltpu.VMEM((32, parents), F32),
            pltpu.VMEM((128, sums), BF16),
            pltpu.VMEM((128, parents), BF16),
            pltpu.VMEM((63, SEPS, 8, CH), F32),
            pltpu.VMEM((31, SEPS, 8, CH), F32),
            pltpu.VMEM((26, SEPS, 8, CH), F32),
            pltpu.VMEM((LEVELS, SEPS, 8, CH), F32),
            pltpu.VMEM((LEVELS, SEPS - 1, 8, CH), F32),
            pltpu.VMEM((63, SEPS, 8, CH), F32),
            pltpu.VMEM((RHS, CH), BF16),
            pltpu.VMEM((SEPS, 8, CH), F32),
            pltpu.VMEM((SEPS, 8, LEVELS * 32), F32),
            pltpu.VMEM((RHS, CH), BF16),
            pltpu.VMEM((RHS, LEVELS * 32), BF16),
            pltpu.VMEM((RHS, 128), F32),
            pltpu.VMEM((2, SEPS - 1, 32, TOP_CHUNKS * CH), F32),
            pltpu.VMEM((2, CH, TOP_CHUNKS * CH), BF16),
            pltpu.VMEM((2, CH, TOP_CHUNKS * CH), BF16),
            pltpu.VMEM((SEPS, 16, 128), F32),
            pltpu.VMEM((2, 16, 8, CH), F32),
            pltpu.VMEM((16, 8, CH), F32),
            pltpu.VMEM((15, 8, CH), F32),
            pltpu.VMEM((2, 16, 8, CH), F32),
            pltpu.VMEM((SEPS, 16, 128), F32),
            pltpu.VMEM((SEPS - 1, 16, 128), F32),
            dma((4,)), dma((4,)), dma((3,)), dma((3,)), dma((16,)), dma((4,)), dma((2,)), dma((3, 3)), dma((7,)),
            dma((11,)),
        ],
        compiler_params=pltpu.CompilerParams(
            collective_id=0, has_side_effects=True, vmem_limit_bytes=60 * 2**20),
        name="forward_substitution",
    )(
        block_mask[0, 0], leaf_rows, leaf_rhs[:, 0, 0, :], leaf_inv[0, 0], sep_rhs[:, 0, 0, :],
        leaf_coupling[0, 0], dinv_rows[0, 0], sep_coupling[0, 0],
    )
    return (leaf_solution[:, None, None, :], sep_solution[:, None, None, :])


def solution(mesh):
    return jax.shard_map(
        body,
        mesh=mesh,
        in_specs=(
            P(None, "leaf", "sep", None),
            P("leaf", "sep", None, None),
            P("leaf", "sep", None, None),
            P("leaf", "sep", None),
            P("leaf", "sep"),
            P(None, "leaf", "sep", None),
            P("leaf", "sep", None, None),
            P("leaf", "sep", None, None),
        ),
        out_specs=(P(None, "leaf", "sep", None), P(None, "leaf", "sep", None)),
        check_vma=False,
    )
```
